512 devices in a mesh: elem: 128 (over y, z, core), lev: 4 (over x).
Axes of the slice: x: 4, y: 8, z: 8, core: 2. Of those that a mesh axis runs over, the one named last changes fastest.
Arguments:
- crm_state: float32 [8, 32, 64, 16384], P(None, None, 'lev', 'elem'), may hold values from -6 to 6
- dyn_state: float32 [8, 32, 16384], P(None, 'lev', 'elem'), may hold values from -6 to 6
- ls_tend: float32 [8, 32, 16384], P(None, 'lev', 'elem'), may hold values from -4 to 4
- span_slot: int32 [16384], P('elem'), may hold values from 0 to 16383, as said below
- neighbours: int32 [4096, 4], P('elem'), may hold values from 0 to 16383, as said below
Outputs:
- crm_next: float32 [8, 32, 64, 16384], P(None, None, 'lev', 'elem')
- dynamics_next: float32 [8, 32, 16384], P(None, 'lev', 'elem')
The draws below stay inside these ranges and needn't reach their ends.
Inputs may be any that keep to these rules, and one draw needn't show every extreme that they name: `span_slot`: every span slot is named by exactly one column; slot // 128 is the span index of elem; from one owner index of elem at most 2 columns go to one span index, and 2 is reached in every draw. `neighbours`: edges are paired both ways; east and west partners lie on the next and previous index of elem, wrapping; south and north partners lie on the same index.
All inputs are finite; a program needn't handle non-finite values.
Results may differ from the reference program's by a relative error of at most 0.00002.
Values sent between devices are 32-bit elements; how exact they have to be, the bound alone decides.
No kernel may reach another device: no remote copies, remote signals or barrier semaphores. Data moves between devices by JAX's collectives and lax.ppermute only.
A program may use at most 64 MiB of HBM per device.

```python
import jax
import jax.numpy as jnp
from jax import lax

FIELDS = 8
LEV = 32
CRMX = 64
SUBSTEPS = 2
SAT_ITERS = 3
COL_DEV = 128
ELEM_DEV = 32
COLUMNS = 16384
ELEMENTS = 4096
CAP = 2


def draw_span_slot(key, part):
    key = jax.random.fold_in(key, 11)
    key_offset, key_roles, key_slots = jax.random.split(key, 3)
    owners = COLUMNS // COL_DEV
    ranks = jnp.arange(COL_DEV, dtype=jnp.int32)
    half_count = COL_DEV // 2
    groups_of = jnp.where(ranks < half_count, ranks // CAP, half_count // CAP + (ranks - half_count) // (CAP // 2))
    base = jax.random.permutation(key_offset, owners).astype(jnp.int32)
    ids = jnp.arange(owners, dtype=jnp.int32)
    scores = jnp.where(ids == owners // 2, -3, jnp.where(ids == 1, -2, jnp.where(ids == owners - 1, -1, base)))
    ordered = jnp.argsort(scores, stable=True).astype(jnp.int32)
    offsets = ordered[groups_of]
    roles = jax.vmap(lambda k: jax.random.permutation(k, COL_DEV))(jax.random.split(key_roles, owners))
    sources = jnp.arange(owners, dtype=jnp.int32)[:, None]
    target = (sources + offsets[roles]) % owners
    slot_perm = jax.vmap(lambda k: jax.random.permutation(k, COL_DEV))(jax.random.split(key_slots, owners))
    slot_index = slot_perm[target, roles]
    return (target * COL_DEV + slot_index).reshape(-1).astype(jnp.int32)


def draw_neighbours(key, part):
    key = jax.random.fold_in(key, 23)
    key_east, key_south = jax.random.split(key)
    blocks_n = ELEMENTS // ELEM_DEV
    east_perm = jax.vmap(lambda k: jax.random.permutation(k, ELEM_DEV))(jax.random.split(key_east, blocks_n))
    south_perm = jax.vmap(lambda k: jax.random.permutation(k, ELEM_DEV))(jax.random.split(key_south, blocks_n))
    west_inv = jnp.argsort(east_perm, axis=1).astype(jnp.int32)
    north_inv = jnp.argsort(south_perm, axis=1).astype(jnp.int32)
    blocks = jnp.arange(blocks_n, dtype=jnp.int32)[:, None]
    east_code = ((blocks + 1) % blocks_n * ELEM_DEV + east_perm) * 4 + 3
    west_src = jnp.roll(west_inv, 1, axis=0)
    west_code = ((blocks - 1) % blocks_n * ELEM_DEV + west_src) * 4 + 1
    south_code = (blocks * ELEM_DEV + south_perm) * 4 + 2
    north_code = (blocks * ELEM_DEV + north_inv) * 4 + 0
    return jnp.stack([south_code, east_code, north_code, west_code], axis=-1).reshape(ELEMENTS, 4).astype(jnp.int32)


def level_of(key, dims, pieces, least, high):
    def one(dim, shards_of):
        draws = jax.random.uniform(jax.random.fold_in(jax.random.fold_in(key, 6), dim), (shards_of,), jnp.float32, least / len(pieces), high / len(pieces))
        return jnp.repeat(jnp.exp(draws), dims[dim] // shards_of).reshape((-1,) + (1,) * (len(dims) - dim - 1))

    factor_of = one(*pieces[0])
    for cut in pieces[1:]:
        factor_of = factor_of * one(*cut)
    return factor_of


def centred(rng, shape, spread, bound, shards=(), kind=jnp.bfloat16):
    values = jax.random.normal(rng, shape, jnp.float32) * spread
    if len(shards) > 0:
        values = level_of(rng, shape, shards, -0.22, 0.18) * values
    return jnp.clip(values, min=-bound, max=bound).astype(kind)


def setup_inputs(seed: int = 0) -> dict:
    key_of = jax.random.split(jax.random.key(seed), 6)
    return {
        "crm_state": centred(key_of[0], (FIELDS, LEV, CRMX, COLUMNS), 1.0, 6.0, ((2, 4), (3, 128)), jnp.float32),
        "dyn_state": centred(key_of[1], (FIELDS, LEV, COLUMNS), 1.0, 6.0, ((1, 4), (2, 128)), jnp.float32),
        "ls_tend": centred(key_of[2], (FIELDS, LEV, COLUMNS), 0.5, 4.0, ((1, 4), (2, 128)), jnp.float32),
        "span_slot": draw_span_slot(jax.random.fold_in(key_of[5], 71), 0),
        "neighbours": draw_neighbours(jax.random.fold_in(key_of[5], 71), 0),
    }


DIFFUSE_X = 0.2
DIFFUSE_Z = 0.1
COURANT = 0.3
SAT_SLOPE = 0.3
LATENT = 0.5
RELAX_RATE = 0.5
AUTOCONV = 0.2
BUOYANCY = 0.5
EDGE_WEIGHT = 0.25


def transport(extended):
    centre = extended[:, :, 1:-1]
    eastern = extended[:, :, 2:]
    western = extended[:, :, :-2]
    advect_speed = COURANT * jnp.tanh(centre[0])
    zero_layer = jnp.zeros_like(centre[:, :1])
    upper_cell = jnp.concatenate([centre[:, 1:], zero_layer], axis=1)
    lower_cell = jnp.concatenate([zero_layer, centre[:, :-1]], axis=1)
    return (centre + DIFFUSE_X * (eastern - 2.0 * centre + western)
            - 0.5 * advect_speed * (eastern - western)
            + DIFFUSE_Z * (upper_cell - 2.0 * centre + lower_cell))


def column_physics(fields, forcing):
    wind_u, wind_w, temper, vapour = fields[0], fields[1], fields[2], fields[3]
    cloud_liq, cloud_ice, rain_water, snow_water = fields[4], fields[5], fields[6], fields[7]
    temper_start = temper
    for sweep in range(SAT_ITERS):
        saturated = jnp.exp(SAT_SLOPE * temper)
        change = RELAX_RATE * (vapour - saturated) / (1.0 + LATENT * SAT_SLOPE * saturated)
        change = jnp.maximum(change, -cloud_liq)
        cloud_liq = cloud_liq + change
        vapour = vapour - change
        temper = temper + LATENT * change
    rainout = AUTOCONV * jnp.maximum(cloud_liq, 0.0)
    cloud_liq = cloud_liq - rainout
    rain_water = rain_water + rainout
    snowout = AUTOCONV * jnp.maximum(cloud_ice, 0.0)
    cloud_ice = cloud_ice - snowout
    snow_water = snow_water + snowout
    wind_w = wind_w + BUOYANCY * (temper - temper_start)
    stacked = jnp.stack([wind_u, wind_w, temper, vapour, cloud_liq, cloud_ice, rain_water, snow_water])
    return stacked + forcing


def edge_means(columns):
    field_count, level_count, column_count = columns.shape
    quads = columns.reshape(field_count, level_count, column_count // 4, 4)
    edges = jnp.stack([0.5 * (quads[..., 0] + quads[..., 1]), 0.5 * (quads[..., 1] + quads[..., 3]),
                       0.5 * (quads[..., 2] + quads[..., 3]), 0.5 * (quads[..., 0] + quads[..., 2])], axis=2)
    return quads, edges


def smooth_from(quads, edges, partner):
    jump = partner - edges
    south_west = quads[..., 0] + EDGE_WEIGHT * (jump[:, :, 0] + jump[:, :, 3])
    south_east = quads[..., 1] + EDGE_WEIGHT * (jump[:, :, 0] + jump[:, :, 1])
    north_west = quads[..., 2] + EDGE_WEIGHT * (jump[:, :, 2] + jump[:, :, 3])
    north_east = quads[..., 3] + EDGE_WEIGHT * (jump[:, :, 2] + jump[:, :, 1])
    smoothed = jnp.stack([south_west, south_east, north_west, north_east], axis=-1)
    return smoothed.reshape(quads.shape[0], quads.shape[1], -1)


def reference(crm_state, dyn_state, ls_tend, span_slot, neighbours):
    quads, edges = edge_means(dyn_state)
    flattened = edges.reshape(FIELDS, LEV, 4 * ELEMENTS)
    lookup = ((neighbours % 4) * ELEMENTS + neighbours // 4).T.reshape(-1)
    partner = jnp.take(flattened, lookup, axis=2).reshape(FIELDS, LEV, 4, ELEMENTS)
    smoothed = smooth_from(quads, edges, partner)
    forcing = ls_tend + (smoothed - dyn_state)
    forcing_span = jnp.zeros_like(forcing).at[:, :, span_slot].set(forcing)

    def run_block(block_index):
        start = block_index * COL_DEV
        state = lax.dynamic_slice_in_dim(crm_state, start, COL_DEV, 3)
        pushed = lax.dynamic_slice_in_dim(forcing_span, start, COL_DEV, 2)[:, :, None, :]
        current = state
        for substep in range(SUBSTEPS):
            extended = jnp.concatenate([current[:, :, -1:], current, current[:, :, :1]], axis=2)
            current = column_physics(transport(extended), pushed)
        tendency = (jnp.sum(current, axis=2) - jnp.sum(state, axis=2)) / float(CRMX * SUBSTEPS)
        return current, tendency

    blocks, tendencies = lax.map(run_block, jnp.arange(COLUMNS // COL_DEV, dtype=jnp.int32))
    crm_next = jnp.moveaxis(blocks, 0, 3).reshape(FIELDS, LEV, CRMX, COLUMNS)
    tendency = jnp.moveaxis(tendencies, 0, 2).reshape(FIELDS, LEV, COLUMNS)
    dynamics_next = smoothed + tendency[:, :, span_slot]
    return crm_next, dynamics_next
```

```python
import functools

import jax
import jax.numpy as jnp
from jax import lax
from jax.experimental import pallas as pl
from jax.experimental.pallas import tpu as pltpu
from jax.sharding import PartitionSpec as P

SUBSTEPS = 2
SAT_ITERS = 3
DIFFUSE_X = 0.2
DIFFUSE_Z = 0.1
COURANT = 0.3
SAT_SLOPE = 0.3
LATENT = 0.5
RELAX_RATE = 0.5
AUTOCONV = 0.2
BUOYANCY = 0.5
EDGE_WEIGHT = 0.25
CENTRE = 1.0 - 2.0 * DIFFUSE_X - 2.0 * DIFFUSE_Z

F32 = jnp.float32
BF16 = jnp.bfloat16
VMEM_LIMIT = 40 * 1024 * 1024


def iota(shape, dim):
    return lax.broadcasted_iota(jnp.int32, shape, dim)


def thirds(x):
    high = x.astype(BF16)
    rest = x - high.astype(F32)
    middle = rest.astype(BF16)
    low = (rest - middle.astype(F32)).astype(BF16)
    return high, middle, low


def dot(a, b):
    return lax.dot_general(a, b, (((1,), (0,)), ((), ())), preferred_element_type=F32)


def dot_nt(a, b):
    return lax.dot_general(a, b, (((1,), (1,)), ((), ())), preferred_element_type=F32)


def dot_tn(a, b):
    return lax.dot_general(a, b, (((0,), (0,)), ((), ())), preferred_element_type=F32)


def physics(fields):
    wind_u, wind_w, temper, vapour, cloud_liq, cloud_ice, rain_water, snow_water = fields
    temper_start = temper
    for _ in range(SAT_ITERS):
        saturated = jnp.exp(SAT_SLOPE * temper)
        change = RELAX_RATE * (vapour - saturated) / (1.0 + LATENT * SAT_SLOPE * saturated)
        change = jnp.maximum(change, -cloud_liq)
        cloud_liq = cloud_liq + change
        vapour = vapour - change
        temper = temper + LATENT * change
    rainout = AUTOCONV * jnp.maximum(cloud_liq, 0.0)
    snowout = AUTOCONV * jnp.maximum(cloud_ice, 0.0)
    return [
        wind_u,
        wind_w + BUOYANCY * (temper - temper_start),
        temper,
        vapour,
        cloud_liq - rainout,
        cloud_ice - snowout,
        rain_water + rainout,
        snow_water + snowout,
    ]


def maps_kernel(odd_ref, nb_ref, slot_ref, self_ref, chip_ref, core_ref, send_ref):
    column_count = slot_ref.shape[1]
    elem_local = column_count // 4
    shape = (column_count, column_count)
    row, col = iota(shape, 0), iota(shape, 1)
    row_corner, col_corner = row & 3, col & 3
    spread = (iota((elem_local, column_count), 1) // 4 == iota((elem_local, column_count), 0)).astype(BF16)
    code = nb_ref[...]
    high = dot((code >> 7).astype(F32).astype(BF16), spread)
    low = dot((code & 127).astype(F32).astype(BF16), spread)
    code = (high * 128.0 + low).astype(jnp.int32)
    corner = iota((1, column_count), 1) & 3
    along_y = jnp.where(corner < 2, code[0:1], code[2:3])
    along_x = jnp.where((corner & 1) == 1, code[1:2], code[3:4])

    def partner(which):
        edge = which & 3
        place = (which >> 2) % elem_local
        touches = jnp.where(
            edge == 0,
            (row_corner < 2).astype(F32),
            jnp.where(
                edge == 1,
                (row_corner & 1).astype(F32),
                jnp.where(edge == 2, (row_corner >= 2).astype(F32), 1.0 - (row_corner & 1).astype(F32)),
            ),
        )
        return jnp.where((row >> 2) == place, touches, 0.0)

    weight = 0.5 * EDGE_WEIGHT
    own = ((row_corner >> 1) == (col_corner >> 1)).astype(F32) + ((row_corner & 1) == (col_corner & 1)).astype(F32)
    own = jnp.where((row >> 2) == (col >> 2), own, 0.0)
    self_ref[...] = (weight * (partner(along_y) - own)).astype(BF16)
    beside = weight * partner(along_x)
    from_core = (col_corner & 1) != odd_ref[0, 0]
    core_ref[...] = jnp.where(from_core, beside, 0.0).astype(BF16)
    chip_ref[...] = jnp.where(from_core, 0.0, beside).astype(BF16)

    goes = row == slot_ref[...] // column_count
    onehot = goes.astype(F32).astype(BF16)
    rank = jnp.sum(jnp.where(row < col, dot_tn(onehot, onehot), 0.0), axis=0, keepdims=True)
    send_ref[0:column_count] = jnp.where(rank < 0.5, goes.astype(F32), 0.0).astype(BF16)
    send_ref[column_count:] = jnp.where(rank > 0.5, goes.astype(F32), 0.0).astype(BF16)


def forcing_kernel(dyn_ref, chip_ref, core_ref, ls_ref, slot_ref, mself, mchip, mcore, send_ref, out_ref, smooth_ref):
    rows, column_count = dyn_ref.shape
    dyn = dyn_ref[...]

    def through(value, matrix):
        return dot(jnp.concatenate(thirds(value), axis=0), matrix[...])

    change = through(dyn, mself) + through(core_ref[...], mcore) + through(chip_ref[...], mchip)
    change = change[0:rows] + change[rows : 2 * rows] + change[2 * rows :]
    smooth_ref[...] = dyn + change
    slot = ((slot_ref[...] % column_count) + 1).astype(F32)
    rest = column_count - rows
    extra = jnp.where(iota((rest, column_count), 0) == 0, slot, 0.0).astype(BF16)
    empty = jnp.zeros((rest, column_count), BF16)
    high, middle, low = thirds(ls_ref[...] + change)
    send = send_ref[...]
    message = (
        dot_nt(send, jnp.concatenate([high, extra], axis=0))
        + dot_nt(send, jnp.concatenate([middle, empty], axis=0))
        + dot_nt(send, jnp.concatenate([low, empty], axis=0))
    )
    spans = message.shape[0] // 2
    out_ref[:, 0, :] = message[0:spans]
    out_ref[:, 1, :] = message[spans:]


def place_kernel(got_ref, out_ref, slots_ref):
    copies, rows, column_count = out_ref.shape
    got = jnp.concatenate([got_ref[:, 0, :], got_ref[:, 1, :]], axis=0)
    slot = got[:, rows : rows + 1] - 1.0
    lanes = iota((got.shape[0], column_count), 1).astype(F32)
    slots = (lanes == slot).astype(F32).astype(BF16)
    slots_ref[...] = slots
    high, middle, low = thirds(got)
    placed = (dot_tn(high, slots) + dot_tn(middle, slots) + dot_tn(low, slots))[0:rows]
    for copy in range(copies):
        out_ref[copy] = placed


def edges_kernel(crm_ref, left_ref, right_ref):
    cells, levels = 16, left_ref.shape[2]
    for f in range(left_ref.shape[1]):
        for j in range(2):
            left_ref[j, f] = crm_ref[f, pl.ds(j, levels, stride=cells), :]
            right_ref[j, f] = crm_ref[f, pl.ds(cells - 2 + j, levels, stride=cells), :]


def first_kernel(crm_ref, left_ref, right_ref, own_left, own_right, a_ref, b_ref, u_ref, sum_ref, pre_ref, end_ref):
    fields, levels, cells, lanes = crm_ref.shape
    group = 4
    level = iota((levels, lanes), 0)

    def halo(west, centre, east, side):
        speed = 0.5 * COURANT * jnp.tanh(centre[0])
        moved = []
        for f in range(fields):
            up = jnp.where(level < levels - 1, pltpu.roll(centre[f], levels - 1, 0), 0.0)
            down = jnp.where(level > 0, pltpu.roll(centre[f], 1, 0), 0.0)
            moved.append(
                CENTRE * centre[f]
                + DIFFUSE_X * (east[f] + west[f])
                + DIFFUSE_Z * (up + down)
                - speed * (east[f] - west[f])
            )
        for f, value in enumerate(physics(moved)):
            end_ref[side, f] = value

    halo(left_ref[0], left_ref[1], own_left[0], 0)
    halo(own_right[1], right_ref[0], right_ref[1], 1)
    cell = iota((cells, lanes), 0)

    def beside(centre, west_end, east_end):
        west = jnp.where(cell == 0, west_end, pltpu.roll(centre, 1, 0))
        east = jnp.where(cell == cells - 1, east_end, pltpu.roll(centre, cells - 1, 0))
        return west, east

    def vertical(ref, f, k, weight_up, weight_down):
        return weight_up * ref[f, jnp.minimum(k + 1, levels - 1)] + weight_down * ref[f, jnp.maximum(k - 1, 0)]

    def weights(k):
        return jnp.where(k < levels - 1, DIFFUSE_Z, 0.0), jnp.where(k > 0, DIFFUSE_Z, 0.0)

    @pl.loop(0, levels // group)
    def _(step):
        for j in range(group):
            k = step * group + j
            weight_up, weight_down = weights(k)
            moved = []
            for f in range(fields):
                centre = crm_ref[f, k]
                west, east = beside(centre, left_ref[1, f, pl.ds(k, 1), :], right_ref[0, f, pl.ds(k, 1), :])
                if f == 0:
                    speed = 0.5 * COURANT * jnp.tanh(centre)
                sum_ref[f, pl.ds(k, 1), :] = jnp.sum(centre, axis=0, keepdims=True)
                moved.append(
                    CENTRE * centre
                    + DIFFUSE_X * (east + west)
                    + vertical(crm_ref, f, k, weight_up, weight_down)
                    - speed * (east - west)
                )
            for f, value in enumerate(physics(moved)):
                pre_ref[f, k] = value

    @pl.loop(0, levels // group)
    def _(step):
        for j in range(group):
            k = step * group + j
            weight_up, weight_down = weights(k)
            for f in range(fields):
                centre = pre_ref[f, k]
                west, east = beside(centre, end_ref[0, f, pl.ds(k, 1), :], end_ref[1, f, pl.ds(k, 1), :])
                a_ref[f, k] = CENTRE * centre + DIFFUSE_X * (east + west) + vertical(pre_ref, f, k, weight_up, weight_down)
                b_ref[f, k] = (0.5 * COURANT) * (east - west)
                if f == 0:
                    u_ref[k] = centre


def second_kernel(force_ref, a_ref, b_ref, u_ref, sum_ref, out_ref, part_ref, push_ref, shift_ref, next_ref, sems):
    fields, levels, cells, lanes = a_ref.shape
    blocks = force_ref.shape[0]
    share = levels // blocks
    level = iota((levels, lanes), 0)
    for f in range(fields):
        for b in range(blocks):
            push_ref[f, b * share : (b + 1) * share] = force_ref[b, f * share : (f + 1) * share]
    for f in range(fields):
        push = push_ref[f]
        up = jnp.where(level < levels - 1, pltpu.roll(push, levels - 1, 0), 0.0)
        down = jnp.where(level > 0, pltpu.roll(push, 1, 0), 0.0)
        shift_ref[f] = (1.0 - 2.0 * DIFFUSE_Z) * push + DIFFUSE_Z * (up + down)
    group = 4
    copies = []
    for b in range(blocks):

        @pl.loop(0, share // group)
        def _(step):
            for j in range(group):
                within = step * group + j
                k = b * share + within
                push = [push_ref[f, pl.ds(k, 1), :] for f in range(fields)]
                speed = jnp.tanh(u_ref[k] + push[0])
                moved = [
                    a_ref[f, k] + shift_ref[f, pl.ds(k, 1), :] - speed * b_ref[f, k] for f in range(fields)
                ]
                for f, value in enumerate(physics(moved)):
                    value = value + push[f]
                    next_ref[f, k] = value
                    part_ref[b, pl.ds(f * share + within, 1), :] = jnp.sum(value, axis=0, keepdims=True)

        here = pl.ds(b * share, share)
        copy = pltpu.make_async_copy(next_ref.at[:, here], out_ref.at[:, here], sems.at[b])
        copy.start()
        copies.append(copy)
        for f in range(fields):
            at = slice(f * share, (f + 1) * share)
            part_ref[b, at] = part_ref[b, at] - sum_ref[f, b * share : (b + 1) * share]
    for copy in copies:
        copy.wait()


def back_kernel(scale, part_ref, slots_ref, out_ref):
    blocks, rows, lanes = part_ref.shape
    total = part_ref[0]
    for b in range(1, blocks):
        total = total + part_ref[b]
    slots = slots_ref[...]
    message = 0.0
    for term in thirds(total * scale):
        message = message + dot_nt(slots, jnp.concatenate([term, term], axis=0))
    owners = message.shape[0] // 2
    first = iota((owners, 2 * rows), 1) < rows
    out_ref[:, 0, :] = jnp.where(first, message[0:owners], message[owners:])


def final_kernel(got_ref, send_ref, smooth_ref, out_ref):
    rows, columns = smooth_ref.shape
    spans = got_ref.shape[0]
    got = got_ref[:, 0, :]
    first, second = 0.0, 0.0
    for term in thirds(got):
        first = first + dot_tn(term, send_ref[0:spans])
        second = second + dot_tn(term, send_ref[spans:])
    out_ref[...] = smooth_ref[...] + first[0:rows] + second[rows:]


def call(kernel, outs, *args, kept=(), scratch=(), cost=0, name=None):
    vmem = pl.BlockSpec(memory_space=pltpu.VMEM)
    smem = pl.BlockSpec(memory_space=pltpu.SMEM)
    hbm = pl.BlockSpec(memory_space=pl.ANY)
    result = pl.pallas_call(
        kernel,
        out_shape=[s for s, _ in outs],
        in_specs=[smem if i in kept else vmem for i in range(len(args))],
        out_specs=[hbm if place == "hbm" else vmem for _, place in outs],
        scratch_shapes=list(scratch),
        compiler_params=pltpu.CompilerParams(vmem_limit_bytes=VMEM_LIMIT),
        cost_estimate=pl.CostEstimate(flops=cost, bytes_accessed=0, transcendentals=0) if cost else None,
        name=name,
    )(*args)
    return result


def here(*shape, dtype=F32):
    return (pltpu.VMEM(shape, dtype), "vmem")


def there(*shape, dtype=F32):
    return (jax.ShapeDtypeStruct(shape, dtype), "hbm")


def plain(*shape, dtype=F32):
    return (jax.ShapeDtypeStruct(shape, dtype), "vmem")


def per_device(crm_state, dyn_state, ls_tend, span_slot, neighbours):
    elem_count = lax.axis_size("elem")
    lev_count = lax.axis_size("lev")
    fields, share, columns = dyn_state.shape
    _, levels, cells, _ = crm_state.shape
    rows = fields * share
    dyn = dyn_state.reshape(rows, columns)
    tend = ls_tend.reshape(rows, columns)
    slot = span_slot.reshape(1, columns)

    core_pairs = [(i, i ^ 1) for i in range(elem_count)]
    chip_pairs = [(i, ((i ^ 1) + (2 if i & 1 else -2)) % elem_count) for i in range(elem_count)]
    from_chip = lax.ppermute(dyn, "elem", chip_pairs)
    from_core = lax.ppermute(dyn, "elem", core_pairs)

    left, right = call(
        edges_kernel,
        [plain(2, fields, levels, columns)] * 2,
        crm_state.reshape(fields, levels * cells, columns),
        name="block_edges",
    )
    ring = [(i, (i + 1) % lev_count) for i in range(lev_count)]
    from_left = lax.ppermute(right, "lev", ring)
    from_right = lax.ppermute(left, "lev", [(j, i) for i, j in ring])

    odd = (lax.axis_index("elem") & 1).astype(jnp.int32).reshape(1, 1)
    square = here(columns, columns, dtype=BF16)
    mself, mchip, mcore, send = call(
        maps_kernel,
        [square, square, square, here(2 * elem_count, columns, dtype=BF16)],
        odd,
        neighbours.T,
        slot,
        kept=(0,),
        name="maps",
    )
    message, smoothed = call(
        forcing_kernel,
        [plain(elem_count, 2, columns), here(rows, columns)],
        dyn,
        from_chip,
        from_core,
        tend,
        slot,
        mself,
        mchip,
        mcore,
        send,
        name="forcing",
    )
    got = lax.all_to_all(message, "elem", split_axis=0, concat_axis=0, tiled=True)

    block = (fields, levels, cells, columns)
    base, slope, wind, total = call(
        first_kernel,
        [here(*block), here(*block), here(*block[1:]), here(fields, levels, columns)],
        crm_state,
        from_left,
        from_right,
        left,
        right,
        scratch=[pltpu.VMEM(block, F32), pltpu.VMEM((2, fields, levels, columns), F32)],
        name="first_substep",
    )

    placed, slots = call(
        place_kernel,
        [plain(lev_count, rows, columns), here(2 * elem_count, columns, dtype=BF16)],
        got,
        name="place",
    )
    force = lax.all_to_all(placed, "lev", split_axis=0, concat_axis=0, tiled=True)
    crm_next, parts = call(
        second_kernel,
        [there(*block), plain(lev_count, rows, columns)],
        force,
        base,
        slope,
        wind,
        total,
        scratch=[
            pltpu.VMEM((fields, levels, columns), F32),
            pltpu.VMEM((fields, levels, columns), F32),
            pltpu.VMEM(block, F32),
            pltpu.SemaphoreType.DMA((lev_count,)),
        ],
        name="second_substep",
    )
    parts = lax.all_to_all(parts, "lev", split_axis=0, concat_axis=0, tiled=True)
    scale = 1.0 / (cells * lev_count * SUBSTEPS)
    (answer,) = call(
        functools.partial(back_kernel, scale),
        [plain(elem_count, 1, 2 * rows)],
        parts,
        slots,
        name="back",
    )
    back = lax.all_to_all(answer, "elem", split_axis=0, concat_axis=0, tiled=True)
    (dynamics,) = call(final_kernel, [plain(rows, columns)], back, send, smoothed, name="final")
    return crm_next, dynamics.reshape(fields, share, columns)


def solution(mesh):
    return jax.shard_map(
        per_device,
        mesh=mesh,
        in_specs=(
            P(None, None, "lev", "elem"),
            P(None, "lev", "elem"),
            P(None, "lev", "elem"),
            P("elem"),
            P("elem", None),
        ),
        out_specs=(P(None, None, "lev", "elem"), P(None, "lev", "elem")),
        check_vma=False,
    )
```

```python
import functools

import jax
import jax.numpy as jnp
from jax import lax
from jax.experimental import pallas as pl
from jax.experimental.pallas import tpu as pltpu
from jax.sharding import PartitionSpec as P

SUBSTEPS = 2
SAT_ITERS = 3
DIFFUSE_X = 0.2
DIFFUSE_Z = 0.1
COURANT = 0.3
SAT_SLOPE = 0.3
LATENT = 0.5
RELAX_RATE = 0.5
AUTOCONV = 0.2
BUOYANCY = 0.5
EDGE_WEIGHT = 0.25
CENTRE = 1.0 - 2.0 * DIFFUSE_X - 2.0 * DIFFUSE_Z

PAD = 8

F32 = jnp.float32
BF16 = jnp.bfloat16


def iota(shape, dim):
    return lax.broadcasted_iota(jnp.int32, shape, dim)


def thirds(x):
    high = x.astype(BF16)
    rest = x - high.astype(F32)
    middle = rest.astype(BF16)
    low = (rest - middle.astype(F32)).astype(BF16)
    return high, middle, low


def dot(a, b):
    return lax.dot_general(a, b, (((1,), (0,)), ((), ())), preferred_element_type=F32)


def dot_nt(a, b):
    return lax.dot_general(a, b, (((1,), (1,)), ((), ())), preferred_element_type=F32)


def dot_tn(a, b):
    return lax.dot_general(a, b, (((0,), (0,)), ((), ())), preferred_element_type=F32)


def physics(fields):
    wind_u, wind_w, temper, vapour, cloud_liq, cloud_ice, rain_water, snow_water = fields
    temper_start = temper
    for _ in range(SAT_ITERS):
        saturated = jnp.exp(SAT_SLOPE * temper)
        change = RELAX_RATE * (vapour - saturated) / (1.0 + LATENT * SAT_SLOPE * saturated)
        change = jnp.maximum(change, -cloud_liq)
        cloud_liq = cloud_liq + change
        vapour = vapour - change
        temper = temper + LATENT * change
    rainout = AUTOCONV * jnp.maximum(cloud_liq, 0.0)
    snowout = AUTOCONV * jnp.maximum(cloud_ice, 0.0)
    return [
        wind_u,
        wind_w + BUOYANCY * (temper - temper_start),
        temper,
        vapour,
        cloud_liq - rainout,
        cloud_ice - snowout,
        rain_water + rainout,
        snow_water + snowout,
    ]


def maps(odd_ref, nb_ref, slot_ref, self_ref, chip_ref, core_ref, send_ref):
    column_count = slot_ref.shape[1]
    elem_local = column_count // 4
    shape = (column_count, column_count)
    row, col = iota(shape, 0), iota(shape, 1)
    row_corner, col_corner = row & 3, col & 3
    spread = (iota((elem_local, column_count), 1) // 4 == iota((elem_local, column_count), 0)).astype(BF16)
    code = nb_ref[...]
    high = dot((code >> 7).astype(F32).astype(BF16), spread)
    low = dot((code & 127).astype(F32).astype(BF16), spread)
    code = (high * 128.0 + low).astype(jnp.int32)
    corner = iota((1, column_count), 1) & 3
    along_y = jnp.where(corner < 2, code[0:1], code[2:3])
    along_x = jnp.where((corner & 1) == 1, code[1:2], code[3:4])

    def partner(which):
        edge = which & 3
        place = (which >> 2) % elem_local
        touches = jnp.where(
            edge == 0,
            (row_corner < 2).astype(F32),
            jnp.where(
                edge == 1,
                (row_corner & 1).astype(F32),
                jnp.where(edge == 2, (row_corner >= 2).astype(F32), 1.0 - (row_corner & 1).astype(F32)),
            ),
        )
        return jnp.where((row >> 2) == place, touches, 0.0)

    weight = 0.5 * EDGE_WEIGHT
    own = ((row_corner >> 1) == (col_corner >> 1)).astype(F32) + ((row_corner & 1) == (col_corner & 1)).astype(F32)
    own = jnp.where((row >> 2) == (col >> 2), own, 0.0)
    self_ref[...] = (weight * (partner(along_y) - own)).astype(BF16)
    beside = weight * partner(along_x)
    from_core = (col_corner & 1) != odd_ref[0, 0]
    core_ref[...] = jnp.where(from_core, beside, 0.0).astype(BF16)
    chip_ref[...] = jnp.where(from_core, 0.0, beside).astype(BF16)

    goes = row == slot_ref[...] // column_count
    onehot = goes.astype(F32).astype(BF16)
    rank = jnp.sum(jnp.where(row < col, dot_tn(onehot, onehot), 0.0), axis=0, keepdims=True)
    send_ref[0:column_count] = jnp.where(rank < 0.5, goes.astype(F32), 0.0).astype(BF16)
    send_ref[column_count:] = jnp.where(rank > 0.5, goes.astype(F32), 0.0).astype(BF16)


def forcing_kernel(dyn_ref, chip_ref, core_ref, ls_ref, slot_ref, mself, mchip, mcore, send_ref, out_ref, smooth_ref):
    rows, column_count = dyn_ref.shape
    dyn = dyn_ref[...]

    def through(value, matrix):
        return dot(jnp.concatenate(thirds(value), axis=0), matrix[...])

    change = through(dyn, mself) + through(core_ref[...], mcore) + through(chip_ref[...], mchip)
    change = change[0:rows] + change[rows : 2 * rows] + change[2 * rows :]
    smooth_ref[...] = dyn + change
    slot = ((slot_ref[...] % column_count) + 1).astype(F32)
    rest = column_count - rows
    extra = jnp.where(iota((rest, column_count), 0) == 0, slot, 0.0).astype(BF16)
    empty = jnp.zeros((rest, column_count), BF16)
    high, middle, low = thirds(ls_ref[...] + change)
    send = send_ref[...]
    message = (
        dot_nt(send, jnp.concatenate([high, extra], axis=0))
        + dot_nt(send, jnp.concatenate([middle, empty], axis=0))
        + dot_nt(send, jnp.concatenate([low, empty], axis=0))
    )
    spans = message.shape[0] // 2
    out_ref[:, 0, :] = message[0:spans]
    out_ref[:, 1, :] = message[spans:]


def place_kernel(got_ref, out_ref, slots_ref):
    copies, rows, column_count = out_ref.shape
    got = jnp.concatenate([got_ref[:, 0, :], got_ref[:, 1, :]], axis=0)
    slot = got[:, rows : rows + 1] - 1.0
    lanes = iota((got.shape[0], column_count), 1).astype(F32)
    slots = (lanes == slot).astype(F32).astype(BF16)
    slots_ref[...] = slots
    high, middle, low = thirds(got)
    placed = (dot_tn(high, slots) + dot_tn(middle, slots) + dot_tn(low, slots))[0:rows]
    for copy in range(copies):
        out_ref[copy] = placed


def early_kernel(
    cells, odd_ref, nb_hbm, slot_hbm, dyn_hbm, tend_hbm, crm_hbm,
    self_ref, chip_ref, core_ref, send_ref, left_ref, right_ref, dyn_ref, tend_ref, slot_ref, nb_ref, crm_ref, sems,
):
    pairs = [(slot_hbm, slot_ref), (nb_hbm, nb_ref), (crm_hbm, crm_ref), (dyn_hbm, dyn_ref), (tend_hbm, tend_ref)]
    copies = [pltpu.make_async_copy(source, target, sems.at[i]) for i, (source, target) in enumerate(pairs)]
    for copy in copies:
        copy.start()
    copies[0].wait()
    copies[1].wait()
    maps(odd_ref, nb_ref, slot_ref, self_ref, chip_ref, core_ref, send_ref)
    copies[2].wait()
    levels = left_ref.shape[2]
    for f in range(left_ref.shape[1]):
        for j in range(2):
            left_ref[j, f] = crm_ref[f, pl.ds(j, levels, stride=cells), :]
            right_ref[j, f] = crm_ref[f, pl.ds(cells - 2 + j, levels, stride=cells), :]
    copies[3].wait()
    copies[4].wait()


def stack(ref, f, first, group, cells, levels):
    def level(k):
        return ref[f, pl.ds(pl.multiple_of(PAD + k * cells, 8), cells), :]

    below = jnp.where(first > 0, 1.0, 0.0) * level(jnp.maximum(first - 1, 0))
    above = jnp.where(first + group < levels, 1.0, 0.0) * level(jnp.minimum(first + group, levels - 1))
    west = [ref[f, pl.ds(PAD - 1 + (first + j) * cells, cells), :] for j in range(group)]
    east = [ref[f, pl.ds(PAD + 1 + (first + j) * cells, cells), :] for j in range(group)]
    return [below] + [level(first + j) for j in range(group)] + [above], west, east


def beside(west, east, west_end, east_end):
    cells = west.shape[0]
    cell = iota(west.shape, 0)
    return jnp.where(cell == 0, west_end, west), jnp.where(cell == cells - 1, east_end, east)


def vertical(value):
    levels = value.shape[0]
    level = iota(value.shape, 0)
    up = jnp.where(level < levels - 1, pltpu.roll(value, levels - 1, 0), 0.0)
    down = jnp.where(level > 0, pltpu.roll(value, 1, 0), 0.0)
    return up + down


def folded(value):
    total = value[0:8]
    for i in range(8, value.shape[0], 8):
        total = total + value[i : i + 8]
    return total


def over_rows(ref, f, levels):
    total = ref[f, pl.ds(0, levels, stride=8), :]
    for i in range(1, 8):
        total = total + ref[f, pl.ds(i, levels, stride=8), :]
    return total


def first_kernel(crm_hbm, left_ref, right_ref, pre_ref, end_ref, crm_ref, fold_ref, sems):
    fields, levels, _ = end_ref.shape[1:]
    cells = crm_hbm.shape[1] // levels
    blocks = sems.shape[0]
    share = levels // blocks
    group = 4
    reads = []
    for b in range(blocks):
        size = share * cells
        target = crm_ref.at[:, pl.ds(PAD + b * size, size)]
        reads.append(pltpu.make_async_copy(crm_hbm.at[:, pl.ds(b * size, size)], target, sems.at[b]))
        reads[b].start()
    reads[0].wait()
    for b in range(blocks):
        if b + 1 < blocks:
            reads[b + 1].wait()

        @pl.loop(0, share // group)
        def _(step):
            first = b * share + step * group
            stacks = [stack(crm_ref, f, first, group, cells, levels) for f in range(fields)]
            for j in range(group):
                k = first + j
                at = pl.ds(pl.multiple_of(PAD + k * cells, 8), cells)
                speed = 0.5 * COURANT * jnp.tanh(stacks[0][0][j + 1])
                moved = []
                for f in range(fields):
                    down, centre, up = stacks[f][0][j : j + 3]
                    west, east = beside(
                        stacks[f][1][j],
                        stacks[f][2][j],
                        left_ref[1, f, pl.ds(k, 1), :],
                        right_ref[0, f, pl.ds(k, 1), :],
                    )
                    fold_ref[f, pl.ds(pl.multiple_of(k * 8, 8), 8), :] = folded(centre)
                    moved.append(
                        CENTRE * centre + DIFFUSE_X * (east + west) + DIFFUSE_Z * (up + down) - speed * (east - west)
                    )
                for f, value in enumerate(physics(moved)):
                    pre_ref[f, at, :] = value

    def halo(west, centre, east, side):
        speed = 0.5 * COURANT * jnp.tanh(centre[0])
        moved = [
            CENTRE * centre[f]
            + DIFFUSE_X * (east[f] + west[f])
            + DIFFUSE_Z * vertical(centre[f])
            - speed * (east[f] - west[f])
            for f in range(fields)
        ]
        for f, value in enumerate(physics(moved)):
            end_ref[side, f] = value

    def column(cell):
        return [crm_ref[f, pl.ds(PAD + cell, levels, stride=cells), :] for f in range(fields)]

    halo(left_ref[0], left_ref[1], column(0), 0)
    halo(column(cells - 1), right_ref[0], right_ref[1], 1)
    for f in range(fields):
        end_ref[2, f] = over_rows(fold_ref, f, levels)


def second_kernel(force_ref, pre_ref, end_ref, out_ref, part_ref, push_ref, shift_ref, next_ref, fold_ref, sems):
    fields, levels, _ = end_ref.shape[1:]
    cells = next_ref.shape[1] // levels
    blocks = force_ref.shape[0]
    share = levels // blocks
    group = 4
    for f in range(fields):
        for b in range(blocks):
            push_ref[f, b * share : (b + 1) * share] = force_ref[b, f * share : (f + 1) * share]
    for f in range(fields):
        push = push_ref[f]
        shift_ref[f] = (1.0 - 2.0 * DIFFUSE_Z) * push + DIFFUSE_Z * vertical(push)
    copies = []
    for b in range(blocks):

        @pl.loop(0, share // group)
        def _(step):
            first = b * share + step * group
            stacks = [stack(pre_ref, f, first, group, cells, levels) for f in range(fields)]
            for j in range(group):
                k = first + j
                push = [push_ref[f, pl.ds(k, 1), :] for f in range(fields)]
                speed = 0.5 * COURANT * jnp.tanh(stacks[0][0][j + 1] + push[0])
                moved = []
                for f in range(fields):
                    down, centre, up = stacks[f][0][j : j + 3]
                    west, east = beside(
                        stacks[f][1][j], stacks[f][2][j], end_ref[0, f, pl.ds(k, 1), :], end_ref[1, f, pl.ds(k, 1), :]
                    )
                    moved.append(
                        (CENTRE * centre + shift_ref[f, pl.ds(k, 1), :])
                        + DIFFUSE_X * (east + west)
                        + DIFFUSE_Z * (up + down)
                        - speed * (east - west)
                    )
                for f, value in enumerate(physics(moved)):
                    value = value + push[f]
                    next_ref[f, pl.ds(pl.multiple_of(k * cells, 8), cells), :] = value
                    fold_ref[f, pl.ds(pl.multiple_of(k * 8, 8), 8), :] = folded(value)

        here = pl.ds(b * share * cells, share * cells)
        copy = pltpu.make_async_copy(next_ref.at[:, here], out_ref.at[:, here], sems.at[b])
        copy.start()
        copies.append(copy)
    for f in range(fields):
        change = over_rows(fold_ref, f, levels) - end_ref[2, f]
        for b in range(blocks):
            part_ref[b, f * share : (f + 1) * share] = change[b * share : (b + 1) * share]
    for copy in copies:
        copy.wait()


def back_kernel(scale, part_ref, slots_ref, out_ref):
    blocks, rows, lanes = part_ref.shape
    total = part_ref[0]
    for b in range(1, blocks):
        total = total + part_ref[b]
    slots = slots_ref[...]
    message = 0.0
    for term in thirds(total * scale):
        message = message + dot_nt(slots, jnp.concatenate([term, term], axis=0))
    owners = message.shape[0] // 2
    first = iota((owners, 2 * rows), 1) < rows
    out_ref[:, 0, :] = jnp.where(first, message[0:owners], message[owners:])


def final_kernel(got_ref, send_ref, smooth_ref, out_ref):
    rows, columns = smooth_ref.shape
    spans = got_ref.shape[0]
    got = got_ref[:, 0, :]
    first, second = 0.0, 0.0
    for term in thirds(got):
        first = first + dot_tn(term, send_ref[0:spans])
        second = second + dot_tn(term, send_ref[spans:])
    out_ref[...] = smooth_ref[...] + first[0:rows] + second[rows:]


def call(kernel, outs, *args, scalars=(), far=(), scratch=(), limit=4, name=None):
    vmem = pl.BlockSpec(memory_space=pltpu.VMEM)
    smem = pl.BlockSpec(memory_space=pltpu.SMEM)
    hbm = pl.BlockSpec(memory_space=pltpu.HBM)
    args = [pltpu.with_memory_space_constraint(a, pltpu.HBM) if i in far else a for i, a in enumerate(args)]
    return pl.pallas_call(
        kernel,
        out_shape=[s for s, _ in outs],
        in_specs=[smem if i in scalars else hbm if i in far else vmem for i in range(len(args))],
        out_specs=[hbm if distant else vmem for _, distant in outs],
        scratch_shapes=list(scratch),
        compiler_params=pltpu.CompilerParams(vmem_limit_bytes=limit * 1024 * 1024),
        name=name,
    )(*args)


def near(*shape, dtype=F32):
    return (jax.ShapeDtypeStruct(shape, dtype), False)


def there(*shape, dtype=F32):
    return (pltpu.HBM(shape, dtype), True)


def per_device(crm_state, dyn_state, ls_tend, span_slot, neighbours):
    elem_count = lax.axis_size("elem")
    lev_count = lax.axis_size("lev")
    fields, share, columns = dyn_state.shape
    _, levels, cells, _ = crm_state.shape
    rows = fields * share
    dyn = dyn_state.reshape(rows, columns)
    tend = ls_tend.reshape(rows, columns)
    slot = span_slot.reshape(1, columns)
    crm_flat = crm_state.reshape(fields, levels * cells, columns)
    dma = pltpu.SemaphoreType.DMA

    core_pairs = [(i, i ^ 1) for i in range(elem_count)]
    chip_pairs = [(i, ((i ^ 1) + (2 if i & 1 else -2)) % elem_count) for i in range(elem_count)]
    from_chip = lax.ppermute(dyn, "elem", chip_pairs)
    from_core = lax.ppermute(dyn, "elem", core_pairs)

    odd = (lax.axis_index("elem") & 1).astype(jnp.int32).reshape(1, 1)
    square = near(columns, columns, dtype=BF16)
    edge = near(2, fields, levels, columns)
    mself, mchip, mcore, send, left, right, dyn_near, tend_near, slot_near = call(
        functools.partial(early_kernel, cells),
        [
            square,
            square,
            square,
            near(2 * elem_count, columns, dtype=BF16),
            edge,
            edge,
            near(rows, columns),
            near(rows, columns),
            near(1, columns, dtype=jnp.int32),
        ],
        odd,
        neighbours.T,
        slot,
        dyn,
        tend,
        crm_flat,
        scalars=(0,),
        far=(1, 2, 3, 4, 5),
        scratch=[
            pltpu.VMEM((4, columns // 4), jnp.int32),
            pltpu.VMEM((fields, levels * cells, columns), F32),
            dma((5,)),
        ],
        limit=6,
        name="early",
    )
    message, smoothed = call(
        forcing_kernel,
        [near(elem_count, 2, columns), near(rows, columns)],
        dyn_near,
        from_chip,
        from_core,
        tend_near,
        slot_near,
        mself,
        mchip,
        mcore,
        send,
        name="forcing",
    )
    got = lax.all_to_all(message, "elem", split_axis=0, concat_axis=0, tiled=True)

    ring = [(i, (i + 1) % lev_count) for i in range(lev_count)]
    from_left = lax.ppermute(right, "lev", ring)
    from_right = lax.ppermute(left, "lev", [(j, i) for i, j in ring])
    block = (fields, levels * cells, columns)
    padded = (fields, levels * cells + 2 * PAD, columns)
    eighths = (fields, levels * 8, columns)
    pre, ends = call(
        first_kernel,
        [near(*padded), near(3, fields, levels, columns)],
        crm_flat,
        from_left,
        from_right,
        far=(0,),
        scratch=[pltpu.VMEM(padded, F32), pltpu.VMEM(eighths, F32), dma((lev_count,))],
        limit=8,
        name="first_substep",
    )

    placed, slots = call(
        place_kernel,
        [near(lev_count, rows, columns), near(2 * elem_count, columns, dtype=BF16)],
        got,
        name="place",
    )
    force = lax.all_to_all(placed, "lev", split_axis=0, concat_axis=0, tiled=True)
    crm_next, parts = call(
        second_kernel,
        [there(*block), near(lev_count, rows, columns)],
        force,
        pre,
        ends,
        scratch=[
            pltpu.VMEM((fields, levels, columns), F32),
            pltpu.VMEM((fields, levels, columns), F32),
            pltpu.VMEM(block, F32),
            pltpu.VMEM(eighths, F32),
            dma((lev_count,)),
        ],
        limit=8,
        name="second_substep",
    )
    parts = lax.all_to_all(parts, "lev", split_axis=0, concat_axis=0, tiled=True)
    scale = 1.0 / (cells * lev_count * SUBSTEPS)
    (answer,) = call(
        functools.partial(back_kernel, scale),
        [near(elem_count, 1, 2 * rows)],
        parts,
        slots,
        name="back",
    )
    back = lax.all_to_all(answer, "elem", split_axis=0, concat_axis=0, tiled=True)
    (dynamics,) = call(final_kernel, [near(rows, columns)], back, send, smoothed, name="final")
    return crm_next.reshape(crm_state.shape), dynamics.reshape(fields, share, columns)


def solution(mesh):
    return jax.shard_map(
        per_device,
        mesh=mesh,
        in_specs=(
            P(None, None, "lev", "elem"),
            P(None, "lev", "elem"),
            P(None, "lev", "elem"),
            P("elem"),
            P("elem", None),
        ),
        out_specs=(P(None, None, "lev", "elem"), P(None, "lev", "elem")),
        check_vma=False,
    )
```

```python
import functools

import jax
import jax.numpy as jnp
from jax import lax
from jax.experimental import pallas as pl
from jax.experimental.pallas import tpu as pltpu
from jax.sharding import PartitionSpec as P

SUBSTEPS = 2
SAT_ITERS = 3
DIFFUSE_X = 0.2
DIFFUSE_Z = 0.1
COURANT = 0.3
SAT_SLOPE = 0.3
LATENT = 0.5
RELAX_RATE = 0.5
AUTOCONV = 0.2
BUOYANCY = 0.5
EDGE_WEIGHT = 0.25
CENTRE = 1.0 - 2.0 * DIFFUSE_X - 2.0 * DIFFUSE_Z

PAD = 8

F32 = jnp.float32
BF16 = jnp.bfloat16


def iota(shape, dim):
    return lax.broadcasted_iota(jnp.int32, shape, dim)


def thirds(x):
    high = x.astype(BF16)
    rest = x - high.astype(F32)
    middle = rest.astype(BF16)
    low = (rest - middle.astype(F32)).astype(BF16)
    return high, middle, low


def dot(a, b):
    return lax.dot_general(a, b, (((1,), (0,)), ((), ())), preferred_element_type=F32)


def dot_nt(a, b):
    return lax.dot_general(a, b, (((1,), (1,)), ((), ())), preferred_element_type=F32)


def dot_tn(a, b):
    return lax.dot_general(a, b, (((0,), (0,)), ((), ())), preferred_element_type=F32)


def physics(fields):
    wind_u, wind_w, temper, vapour, cloud_liq, cloud_ice, rain_water, snow_water = fields
    temper_start = temper
    for _ in range(SAT_ITERS):
        saturated = jnp.exp(SAT_SLOPE * temper)
        change = RELAX_RATE * (vapour - saturated) / (1.0 + LATENT * SAT_SLOPE * saturated)
        change = jnp.maximum(change, -cloud_liq)
        cloud_liq = cloud_liq + change
        vapour = vapour - change
        temper = temper + LATENT * change
    rainout = AUTOCONV * jnp.maximum(cloud_liq, 0.0)
    snowout = AUTOCONV * jnp.maximum(cloud_ice, 0.0)
    return [
        wind_u,
        wind_w + BUOYANCY * (temper - temper_start),
        temper,
        vapour,
        cloud_liq - rainout,
        cloud_ice - snowout,
        rain_water + rainout,
        snow_water + snowout,
    ]


def maps(odd_ref, nb_ref, slot_ref, self_ref, chip_ref, core_ref, send_ref):
    column_count = slot_ref.shape[1]
    elem_local = column_count // 4
    shape = (column_count, column_count)
    row, col = iota(shape, 0), iota(shape, 1)
    row_corner, col_corner = row & 3, col & 3
    spread = (iota((elem_local, column_count), 1) // 4 == iota((elem_local, column_count), 0)).astype(BF16)
    code = nb_ref[...]
    high = dot((code >> 7).astype(F32).astype(BF16), spread)
    low = dot((code & 127).astype(F32).astype(BF16), spread)
    code = (high * 128.0 + low).astype(jnp.int32)
    corner = iota((1, column_count), 1) & 3
    along_y = jnp.where(corner < 2, code[0:1], code[2:3])
    along_x = jnp.where((corner & 1) == 1, code[1:2], code[3:4])

    def partner(which):
        edge = which & 3
        place = (which >> 2) % elem_local
        touches = jnp.where(
            edge == 0,
            (row_corner < 2).astype(F32),
            jnp.where(
                edge == 1,
                (row_corner & 1).astype(F32),
                jnp.where(edge == 2, (row_corner >= 2).astype(F32), 1.0 - (row_corner & 1).astype(F32)),
            ),
        )
        return jnp.where((row >> 2) == place, touches, 0.0)

    weight = 0.5 * EDGE_WEIGHT
    own = ((row_corner >> 1) == (col_corner >> 1)).astype(F32) + ((row_corner & 1) == (col_corner & 1)).astype(F32)
    own = jnp.where((row >> 2) == (col >> 2), own, 0.0)
    self_ref[...] = (weight * (partner(along_y) - own)).astype(BF16)
    beside = weight * partner(along_x)
    from_core = (col_corner & 1) != odd_ref[0, 0]
    core_ref[...] = jnp.where(from_core, beside, 0.0).astype(BF16)
    chip_ref[...] = jnp.where(from_core, 0.0, beside).astype(BF16)

    goes = row == slot_ref[...] // column_count
    onehot = goes.astype(F32).astype(BF16)
    rank = jnp.sum(jnp.where(row < col, dot_tn(onehot, onehot), 0.0), axis=0, keepdims=True)
    send_ref[0:column_count] = jnp.where(rank < 0.5, goes.astype(F32), 0.0).astype(BF16)
    send_ref[column_count:] = jnp.where(rank > 0.5, goes.astype(F32), 0.0).astype(BF16)


def forcing_kernel(
    dyn_ref, chip_ref, core_ref, ls_ref, slot_ref, mself, mchip, mcore, send_ref, _, out_ref, smooth_ref
):
    rows, column_count = dyn_ref.shape
    dyn = dyn_ref[...]

    def through(value, matrix):
        return dot(jnp.concatenate(thirds(value), axis=0), matrix[...])

    change = through(dyn, mself) + through(core_ref[...], mcore) + through(chip_ref[...], mchip)
    change = change[0:rows] + change[rows : 2 * rows] + change[2 * rows :]
    smooth_ref[...] = dyn + change
    slot = ((slot_ref[...] % column_count) + 1).astype(F32)
    rest = column_count - rows
    extra = jnp.where(iota((rest, column_count), 0) == 0, slot, 0.0).astype(BF16)
    empty = jnp.zeros((rest, column_count), BF16)
    high, middle, low = thirds(ls_ref[...] + change)
    send = send_ref[...]
    message = (
        dot_nt(send, jnp.concatenate([high, extra], axis=0))
        + dot_nt(send, jnp.concatenate([middle, empty], axis=0))
        + dot_nt(send, jnp.concatenate([low, empty], axis=0))
    )
    spans = message.shape[0] // 2
    out_ref[:, 0, :] = message[0:spans]
    out_ref[:, 1, :] = message[spans:]


def place_kernel(got_ref, out_ref, slots_ref):
    copies, rows, column_count = out_ref.shape
    got = jnp.concatenate([got_ref[:, 0, :], got_ref[:, 1, :]], axis=0)
    slot = got[:, rows : rows + 1] - 1.0
    lanes = iota((got.shape[0], column_count), 1).astype(F32)
    slots = (lanes == slot).astype(F32).astype(BF16)
    slots_ref[...] = slots
    high, middle, low = thirds(got)
    placed = (dot_tn(high, slots) + dot_tn(middle, slots) + dot_tn(low, slots))[0:rows]
    for copy in range(copies):
        out_ref[copy] = placed


def early_kernel(
    odd_ref, nb_hbm, slot_hbm, dyn_hbm, tend_hbm, crm_hbm,
    self_ref, chip_ref, core_ref, send_ref, dyn_ref, tend_ref, slot_ref, crm_ref, nb_ref, sems,
):
    inside = crm_ref.at[:, pl.ds(PAD, crm_hbm.shape[1])]
    pairs = [(slot_hbm, slot_ref), (nb_hbm, nb_ref), (crm_hbm, inside), (dyn_hbm, dyn_ref), (tend_hbm, tend_ref)]
    copies = [pltpu.make_async_copy(source, target, sems.at[i]) for i, (source, target) in enumerate(pairs)]
    for copy in copies:
        copy.start()
    copies[0].wait()
    copies[1].wait()
    maps(odd_ref, nb_ref, slot_ref, self_ref, chip_ref, core_ref, send_ref)
    for copy in copies[2:]:
        copy.wait()


def edges_kernel(cells, crm_ref, left_hbm, right_hbm, left_ref, right_ref, sems):
    levels = left_ref.shape[2]
    for f in range(left_ref.shape[1]):
        for j in range(2):
            left_ref[j, f] = crm_ref[f, pl.ds(PAD + j, levels, stride=cells), :]
            right_ref[j, f] = crm_ref[f, pl.ds(PAD + cells - 2 + j, levels, stride=cells), :]
    copies = [
        pltpu.make_async_copy(left_ref, left_hbm, sems.at[0]),
        pltpu.make_async_copy(right_ref, right_hbm, sems.at[1]),
    ]
    for copy in copies:
        copy.start()
    for copy in copies:
        copy.wait()


def stack(ref, f, first, group, cells, levels):
    def level(k):
        return ref[f, pl.ds(pl.multiple_of(PAD + k * cells, 8), cells), :]

    below = jnp.where(first > 0, 1.0, 0.0) * level(jnp.maximum(first - 1, 0))
    above = jnp.where(first + group < levels, 1.0, 0.0) * level(jnp.minimum(first + group, levels - 1))
    west = [ref[f, pl.ds(PAD - 1 + (first + j) * cells, cells), :] for j in range(group)]
    east = [ref[f, pl.ds(PAD + 1 + (first + j) * cells, cells), :] for j in range(group)]
    return [below] + [level(first + j) for j in range(group)] + [above], west, east


def beside(west, east, west_end, east_end):
    cells = west.shape[0]
    cell = iota(west.shape, 0)
    return jnp.where(cell == 0, west_end, west), jnp.where(cell == cells - 1, east_end, east)


def shares(wind):
    speed = 0.5 * COURANT * jnp.tanh(wind)
    return DIFFUSE_X - speed, DIFFUSE_X + speed


def vertical(value):
    levels = value.shape[0]
    level = iota(value.shape, 0)
    up = jnp.where(level < levels - 1, pltpu.roll(value, levels - 1, 0), 0.0)
    down = jnp.where(level > 0, pltpu.roll(value, 1, 0), 0.0)
    return up + down


def folded(value):
    total = value[0:8]
    for i in range(8, value.shape[0], 8):
        total = total + value[i : i + 8]
    return total


def over_rows(ref, f, levels):
    total = ref[f, pl.ds(0, levels, stride=8), :]
    for i in range(1, 8):
        total = total + ref[f, pl.ds(i, levels, stride=8), :]
    return total


def first_kernel(cells, _, left_ref, right_ref, state_ref, end_ref, fold_ref, done_ref, old_ref):
    fields, levels, _ = end_ref.shape[1:]
    group = 4

    def column(cell):
        return [state_ref[f, pl.ds(PAD + cell, levels, stride=cells), :] for f in range(fields)]

    ends = [column(cell) for cell in (0, cells - 1)]
    for side in range(2):
        for f in range(fields):
            end_ref[side, f] = ends[side][f]

    def level_at(k, rows=cells):
        return pl.ds(pl.multiple_of(PAD + k * cells, 8), rows)

    old_ref[...] = jnp.zeros(old_ref.shape, F32)

    @pl.loop(0, levels // group)
    def _(step):
        first = step * group
        stacks = [stack(state_ref, f, first, group, cells, levels) for f in range(fields)]
        for j in range(group):
            k = first + j
            from_east, from_west = shares(stacks[0][0][j + 1])
            moved = []
            for f in range(fields):
                down, centre, up = stacks[f][0][j : j + 3]
                if j == 0:
                    down = old_ref[f]
                west, east = beside(
                    stacks[f][1][j], stacks[f][2][j], left_ref[1, f, pl.ds(k, 1), :], right_ref[0, f, pl.ds(k, 1), :]
                )
                fold_ref[f, pl.ds(pl.multiple_of(k * 8, 8), 8), :] = folded(centre)
                moved.append(CENTRE * centre + DIFFUSE_Z * (up + down) + from_east * east + from_west * west)
            for f, value in enumerate(physics(moved)):
                done_ref[f, j * cells : (j + 1) * cells] = value
        for f in range(fields):
            old_ref[f] = state_ref[f, level_at(first + group - 1), :]
            state_ref[f, level_at(first, group * cells), :] = done_ref[f]

    def halo(west, centre, east, side):
        from_east, from_west = shares(centre[0])
        moved = [
            CENTRE * centre[f] + DIFFUSE_Z * vertical(centre[f]) + from_east * east[f] + from_west * west[f]
            for f in range(fields)
        ]
        for f, value in enumerate(physics(moved)):
            end_ref[side, f] = value

    own = [[end_ref[side, f] for f in range(fields)] for side in range(2)]
    halo(left_ref[0], left_ref[1], own[0], 0)
    halo(own[1], right_ref[0], right_ref[1], 1)
    for f in range(fields):
        end_ref[2, f] = over_rows(fold_ref, f, levels)


def second_kernel(
    force_ref, pre_ref, end_ref, out_ref, part_ref, rest_ref, push_ref, shift_ref, next_ref, fold_ref, sems
):
    fields, levels, _ = end_ref.shape[1:]
    cells = out_ref.shape[1] // levels
    blocks = force_ref.shape[0]
    share = levels // blocks
    group = 4
    for f in range(fields):
        for b in range(blocks):
            push_ref[f, b * share : (b + 1) * share] = force_ref[b, f * share : (f + 1) * share]
    for f in range(fields):
        push = push_ref[f]
        shift_ref[f] = (1.0 - 2.0 * DIFFUSE_Z) * push + DIFFUSE_Z * vertical(push)
    copies = []
    for b in range(blocks):

        @pl.loop(0, share // group)
        def _(step):
            first = b * share + step * group
            stacks = [stack(pre_ref, f, first, group, cells, levels) for f in range(fields)]
            for j in range(group):
                k = first + j
                push = [push_ref[f, pl.ds(k, 1), :] for f in range(fields)]
                from_east, from_west = shares(stacks[0][0][j + 1] + push[0])
                moved = []
                for f in range(fields):
                    down, centre, up = stacks[f][0][j : j + 3]
                    west, east = beside(
                        stacks[f][1][j], stacks[f][2][j], end_ref[0, f, pl.ds(k, 1), :], end_ref[1, f, pl.ds(k, 1), :]
                    )
                    moved.append(
                        (CENTRE * centre + shift_ref[f, pl.ds(k, 1), :])
                        + DIFFUSE_Z * (up + down)
                        + from_east * east
                        + from_west * west
                    )
                for f, value in enumerate(physics(moved)):
                    value = value + push[f]
                    if b < blocks - 1:
                        next_ref[f, pl.ds(pl.multiple_of(k * cells, 8), cells), :] = value
                    else:
                        rest_ref[f, pl.ds(pl.multiple_of((k - b * share) * cells, 8), cells), :] = value
                    fold_ref[f, pl.ds(pl.multiple_of(k * 8, 8), 8), :] = folded(value)

        if b == blocks - 1:
            break
        here = pl.ds(b * share * cells, share * cells)
        copy = pltpu.make_async_copy(next_ref.at[:, here], out_ref.at[:, here], sems.at[b])
        copy.start()
        copies.append(copy)
    for f in range(fields):
        change = over_rows(fold_ref, f, levels) - end_ref[2, f]
        for b in range(blocks):
            part_ref[b, f * share : (f + 1) * share] = change[b * share : (b + 1) * share]
    for copy in copies:
        copy.wait()


def back_kernel(scale, part_ref, slots_ref, out_ref):
    blocks, rows, lanes = part_ref.shape
    total = part_ref[0]
    for b in range(1, blocks):
        total = total + part_ref[b]
    slots = slots_ref[...]
    message = 0.0
    for term in thirds(total * scale):
        message = message + dot_nt(slots, jnp.concatenate([term, term], axis=0))
    owners = message.shape[0] // 2
    first = iota((owners, 2 * rows), 1) < rows
    out_ref[:, 0, :] = jnp.where(first, message[0:owners], message[owners:])


def final_kernel(got_ref, send_ref, smooth_ref, rest_ref, _, dyn_hbm, crm_hbm, dyn_ref, sems):
    rows, columns = smooth_ref.shape
    size = rest_ref.shape[1]
    rest = pltpu.make_async_copy(rest_ref, crm_hbm.at[:, pl.ds(crm_hbm.shape[1] - size, size)], sems.at[0])
    rest.start()
    spans = got_ref.shape[0]
    got = got_ref[:, 0, :]
    first, second = 0.0, 0.0
    for term in thirds(got):
        first = first + dot_tn(term, send_ref[0:spans])
        second = second + dot_tn(term, send_ref[spans:])
    dyn_ref[...] = smooth_ref[...] + first[0:rows] + second[rows:]
    copy = pltpu.make_async_copy(dyn_ref, dyn_hbm, sems.at[1])
    copy.start()
    rest.wait()
    copy.wait()


def call(kernel, outs, *args, scalars=(), far=(), scratch=(), same=None, limit=4, name=None):
    vmem = pl.BlockSpec(memory_space=pltpu.VMEM)
    smem = pl.BlockSpec(memory_space=pltpu.SMEM)
    hbm = pl.BlockSpec(memory_space=pltpu.HBM)
    args = [pltpu.with_memory_space_constraint(a, pltpu.HBM) if i in far else a for i, a in enumerate(args)]
    return pl.pallas_call(
        kernel,
        out_shape=[s for s, _ in outs],
        in_specs=[smem if i in scalars else hbm if i in far else vmem for i in range(len(args))],
        out_specs=[hbm if distant else vmem for _, distant in outs],
        scratch_shapes=list(scratch),
        input_output_aliases=same or {},
        compiler_params=pltpu.CompilerParams(vmem_limit_bytes=limit * 1024 * 1024),
        name=name,
    )(*args)


def near(*shape, dtype=F32):
    return (jax.ShapeDtypeStruct(shape, dtype), False)


def there(*shape, dtype=F32):
    return (pltpu.HBM(shape, dtype), True)


def per_device(crm_state, dyn_state, ls_tend, span_slot, neighbours):
    elem_count = lax.axis_size("elem")
    lev_count = lax.axis_size("lev")
    fields, share, columns = dyn_state.shape
    _, levels, cells, _ = crm_state.shape
    rows = fields * share
    dyn = dyn_state.reshape(rows, columns)
    tend = ls_tend.reshape(rows, columns)
    slot = span_slot.reshape(1, columns)
    crm_flat = crm_state.reshape(fields, levels * cells, columns)
    dma = pltpu.SemaphoreType.DMA

    core_pairs = [(i, i ^ 1) for i in range(elem_count)]
    chip_pairs = [(i, ((i ^ 1) + (2 if i & 1 else -2)) % elem_count) for i in range(elem_count)]
    from_chip = lax.ppermute(dyn, "elem", chip_pairs)

    odd = (lax.axis_index("elem") & 1).astype(jnp.int32).reshape(1, 1)
    square = near(columns, columns, dtype=BF16)
    padded = (fields, levels * cells + 2 * PAD, columns)
    mself, mchip, mcore, send, dyn_near, tend_near, slot_near, state = call(
        early_kernel,
        [
            square,
            square,
            square,
            near(2 * elem_count, columns, dtype=BF16),
            near(rows, columns),
            near(rows, columns),
            near(1, columns, dtype=jnp.int32),
            near(*padded),
        ],
        odd,
        neighbours.T,
        slot,
        dyn,
        tend,
        crm_flat,
        scalars=(0,),
        far=(1, 2, 3, 4, 5),
        scratch=[
            pltpu.VMEM((4, columns // 4), jnp.int32),
            dma((5,)),
        ],
        name="early",
    )
    from_core = lax.ppermute(dyn_near, "elem", core_pairs)
    edge = (2, fields, levels, columns)
    left, right = call(
        functools.partial(edges_kernel, cells),
        [there(*edge), there(*edge)],
        state,
        scratch=[pltpu.VMEM(edge, F32), pltpu.VMEM(edge, F32), dma((2,))],
        name="block_edges",
    )
    message, smoothed = call(
        forcing_kernel,
        [near(elem_count, 2, columns), near(rows, columns)],
        dyn_near,
        from_chip,
        from_core,
        tend_near,
        slot_near,
        mself,
        mchip,
        mcore,
        send,
        left,
        far=(9,),
        name="forcing",
    )
    got = lax.all_to_all(message, "elem", split_axis=0, concat_axis=0, tiled=True)

    ring = [(i, (i + 1) % lev_count) for i in range(lev_count)]
    from_left = lax.ppermute(right, "lev", ring)
    from_right = lax.ppermute(left, "lev", [(j, i) for i, j in ring])
    eighths = (fields, levels * 8, columns)
    pre, ends = call(
        functools.partial(first_kernel, cells),
        [near(*padded), near(3, fields, levels, columns)],
        state,
        from_left,
        from_right,
        scratch=[
            pltpu.VMEM(eighths, F32),
            pltpu.VMEM((fields, 4 * cells, columns), F32),
            pltpu.VMEM((fields, cells, columns), F32),
        ],
        same={0: 0},
        limit=8,
        name="first_substep",
    )

    placed, slots = call(
        place_kernel,
        [near(lev_count, rows, columns), near(2 * elem_count, columns, dtype=BF16)],
        got,
        name="place",
    )
    force = lax.all_to_all(placed, "lev", split_axis=0, concat_axis=0, tiled=True)
    size = levels // lev_count * cells
    crm_next, parts, rest = call(
        second_kernel,
        [there(fields, levels * cells, columns), near(lev_count, rows, columns), near(fields, size, columns)],
        force,
        pre,
        ends,
        scratch=[
            pltpu.VMEM((fields, levels, columns), F32),
            pltpu.VMEM((fields, levels, columns), F32),
            pltpu.VMEM((fields, levels * cells - size, columns), F32),
            pltpu.VMEM(eighths, F32),
            dma((lev_count - 1,)),
        ],
        limit=8,
        name="second_substep",
    )
    parts = lax.all_to_all(parts, "lev", split_axis=0, concat_axis=0, tiled=True)
    scale = 1.0 / (cells * lev_count * SUBSTEPS)
    (answer,) = call(
        functools.partial(back_kernel, scale),
        [near(elem_count, 1, 2 * rows)],
        parts,
        slots,
        name="back",
    )
    back = lax.all_to_all(answer, "elem", split_axis=0, concat_axis=0, tiled=True)
    dynamics, crm_next = call(
        final_kernel,
        [there(rows, columns), there(fields, levels * cells, columns)],
        back,
        send,
        smoothed,
        rest,
        crm_next,
        far=(4,),
        scratch=[pltpu.VMEM((rows, columns), F32), dma((2,))],
        same={4: 1},
        name="final",
    )
    return crm_next.reshape(crm_state.shape), dynamics.reshape(fields, share, columns)


def solution(mesh):
    return jax.shard_map(
        per_device,
        mesh=mesh,
        in_specs=(
            P(None, None, "lev", "elem"),
            P(None, "lev", "elem"),
            P(None, "lev", "elem"),
            P("elem"),
            P("elem", None),
        ),
        out_specs=(P(None, None, "lev", "elem"), P(None, "lev", "elem")),
        check_vma=False,
    )
```

```python
import functools

import jax
import jax.numpy as jnp
from jax import lax
from jax.experimental import pallas as pl
from jax.experimental.pallas import tpu as pltpu
from jax.sharding import PartitionSpec as P

SUBSTEPS = 2
SAT_ITERS = 3
DIFFUSE_X = 0.2
DIFFUSE_Z = 0.1
COURANT = 0.3
SAT_SLOPE = 0.3
LOG2_E = 1.4426950408889634
LATENT = 0.5
RELAX_RATE = 0.5
AUTOCONV = 0.2
BUOYANCY = 0.5
EDGE_WEIGHT = 0.25
CENTRE = 1.0 - 2.0 * DIFFUSE_X - 2.0 * DIFFUSE_Z

PAD = 8

F32 = jnp.float32
BF16 = jnp.bfloat16


def iota(shape, dim):
    return lax.broadcasted_iota(jnp.int32, shape, dim)


def thirds(x):
    high = x.astype(BF16)
    rest = x - high.astype(F32)
    middle = rest.astype(BF16)
    low = (rest - middle.astype(F32)).astype(BF16)
    return high, middle, low


def dot(a, b):
    return lax.dot_general(a, b, (((1,), (0,)), ((), ())), preferred_element_type=F32)


def dot_nt(a, b):
    return lax.dot_general(a, b, (((1,), (1,)), ((), ())), preferred_element_type=F32)


def dot_tn(a, b):
    return lax.dot_general(a, b, (((0,), (0,)), ((), ())), preferred_element_type=F32)


def physics(fields):
    wind_u, wind_w, temper, vapour, cloud_liq, cloud_ice, rain_water, snow_water = fields
    temper_start = temper
    for _ in range(SAT_ITERS):
        saturated = jnp.exp2(SAT_SLOPE * LOG2_E * temper)
        change = RELAX_RATE * (vapour - saturated) / (1.0 + LATENT * SAT_SLOPE * saturated)
        change = jnp.maximum(change, -cloud_liq)
        cloud_liq = cloud_liq + change
        vapour = vapour - change
        temper = temper + LATENT * change
    rainout = AUTOCONV * jnp.maximum(cloud_liq, 0.0)
    snowout = AUTOCONV * jnp.maximum(cloud_ice, 0.0)
    return [
        wind_u,
        wind_w + BUOYANCY * (temper - temper_start),
        temper,
        vapour,
        cloud_liq - rainout,
        cloud_ice - snowout,
        rain_water + rainout,
        snow_water + snowout,
    ]


def maps(odd_ref, nb_ref, slot_ref, self_ref, chip_ref, core_ref, send_ref):
    column_count = slot_ref.shape[1]
    elem_local = column_count // 4
    shape = (column_count, column_count)
    row, col = iota(shape, 0), iota(shape, 1)
    row_corner, col_corner = row & 3, col & 3
    spread = (iota((elem_local, column_count), 1) // 4 == iota((elem_local, column_count), 0)).astype(BF16)
    code = nb_ref[...]
    high = dot((code >> 7).astype(F32).astype(BF16), spread)
    low = dot((code & 127).astype(F32).astype(BF16), spread)
    code = (high * 128.0 + low).astype(jnp.int32)
    corner = iota((1, column_count), 1) & 3
    along_y = jnp.where(corner < 2, code[0:1], code[2:3])
    along_x = jnp.where((corner & 1) == 1, code[1:2], code[3:4])

    def partner(which):
        edge = which & 3
        place = (which >> 2) % elem_local
        touches = jnp.where(
            edge == 0,
            (row_corner < 2).astype(F32),
            jnp.where(
                edge == 1,
                (row_corner & 1).astype(F32),
                jnp.where(edge == 2, (row_corner >= 2).astype(F32), 1.0 - (row_corner & 1).astype(F32)),
            ),
        )
        return jnp.where((row >> 2) == place, touches, 0.0)

    weight = 0.5 * EDGE_WEIGHT
    own = ((row_corner >> 1) == (col_corner >> 1)).astype(F32) + ((row_corner & 1) == (col_corner & 1)).astype(F32)
    own = jnp.where((row >> 2) == (col >> 2), own, 0.0)
    self_ref[...] = (weight * (partner(along_y) - own)).astype(BF16)
    beside = weight * partner(along_x)
    from_core = (col_corner & 1) != odd_ref[0, 0]
    core_ref[...] = jnp.where(from_core, beside, 0.0).astype(BF16)
    chip_ref[...] = jnp.where(from_core, 0.0, beside).astype(BF16)

    goes = row == slot_ref[...] // column_count
    onehot = goes.astype(F32).astype(BF16)
    rank = jnp.sum(jnp.where(row < col, dot_tn(onehot, onehot), 0.0), axis=0, keepdims=True)
    send_ref[0:column_count] = jnp.where(rank < 0.5, goes.astype(F32), 0.0).astype(BF16)
    send_ref[column_count:] = jnp.where(rank > 0.5, goes.astype(F32), 0.0).astype(BF16)


def forcing_kernel(
    core_ref, chip_ref, dyn_ref, ls_ref, slot_ref, mself, mchip, mcore, send_ref, _, out_hbm, smooth_ref, out_ref, sems
):
    rows, column_count = dyn_ref.shape
    dyn = dyn_ref[...]

    def through(value, matrix):
        return dot(jnp.concatenate(thirds(value), axis=0), matrix[...])

    change = through(dyn, mself) + through(core_ref[...], mcore) + through(chip_ref[...], mchip)
    change = change[0:rows] + change[rows : 2 * rows] + change[2 * rows :]
    smooth_ref[...] = dyn + change
    slot = ((slot_ref[...] % column_count) + 1).astype(F32)
    rest = column_count - rows
    extra = jnp.where(iota((rest, column_count), 0) == 0, slot, 0.0).astype(BF16)
    empty = jnp.zeros((rest, column_count), BF16)
    high, middle, low = thirds(ls_ref[...] + change)
    terms = [
        jnp.concatenate([high, extra], axis=0),
        jnp.concatenate([middle, empty], axis=0),
        jnp.concatenate([low, empty], axis=0),
    ]
    spans = send_ref.shape[0] // 2
    parts = sems.shape[0]
    size = spans // parts
    copies = []
    for part in range(parts):
        here = slice(part * size, (part + 1) * size)
        send = jnp.concatenate([send_ref[here], send_ref[spans + here.start : spans + here.stop]], axis=0)
        message = dot_nt(send, terms[0]) + dot_nt(send, terms[1]) + dot_nt(send, terms[2])
        out_ref[here, 0, :] = message[0:size]
        out_ref[here, 1, :] = message[size:]
        copies.append(pltpu.make_async_copy(out_ref.at[here], out_hbm.at[here], sems.at[part]))
        copies[part].start()
    for copy in copies:
        copy.wait()


def place_kernel(got_ref, out_hbm, slots_ref, placed_ref, sems):
    count, rows, column_count = out_hbm.shape
    got = jnp.concatenate([got_ref[:, 0, :], got_ref[:, 1, :]], axis=0)
    slot = got[:, rows : rows + 1] - 1.0
    lanes = iota((got.shape[0], column_count), 1).astype(F32)
    slots = (lanes == slot).astype(F32).astype(BF16)
    slots_ref[...] = slots
    placed_ref[...] = sum(dot_tn(term, slots) for term in thirds(got[:, 0:rows]))
    copies = [pltpu.make_async_copy(placed_ref, out_hbm.at[i], sems.at[i]) for i in range(count)]
    for copy in copies:
        copy.start()
    for copy in copies:
        copy.wait()


def maps_kernel(
    odd_ref, nb_hbm, slot_hbm, dyn_hbm, tend_hbm,
    self_ref, chip_ref, core_ref, send_ref, dyn_ref, tend_ref, slot_ref, nb_ref, sems,
):
    pairs = [(slot_hbm, slot_ref), (nb_hbm, nb_ref), (dyn_hbm, dyn_ref), (tend_hbm, tend_ref)]
    copies = [pltpu.make_async_copy(source, target, sems.at[i]) for i, (source, target) in enumerate(pairs)]
    for copy in copies:
        copy.start()
    copies[0].wait()
    copies[1].wait()
    maps(odd_ref, nb_ref, slot_ref, self_ref, chip_ref, core_ref, send_ref)
    for copy in copies[2:]:
        copy.wait()


def state_kernel(cells, whole_ref, crm_ref, left_hbm, right_hbm, left_ref, right_ref, sems):
    fields, size, _ = whole_ref.shape
    levels = left_ref.shape[2]
    for f in range(fields):
        for j in range(2):
            left_ref[j, f] = whole_ref[f, pl.ds(j, levels, stride=cells), :]
            right_ref[j, f] = whole_ref[f, pl.ds(cells - 2 + j, levels, stride=cells), :]
    copies = []
    for i, (near, far) in enumerate(((left_ref, left_hbm), (right_ref, right_hbm))):
        copies.append(pltpu.make_async_copy(near, far, sems.at[i]))
        copies[i].start()
    step = 64

    @pl.loop(0, size // step)
    def _(i):
        for f in range(fields):
            source = pl.ds(pl.multiple_of(i * step, 8), step)
            crm_ref[f, pl.ds(pl.multiple_of(PAD + i * step, 8), step), :] = whole_ref[f, source, :]

    for copy in copies:
        copy.wait()


def stack(ref, f, first, group, cells, levels):
    def level(k):
        return ref[f, pl.ds(pl.multiple_of(PAD + k * cells, 8), cells), :]

    below = jnp.where(first > 0, 1.0, 0.0) * level(jnp.maximum(first - 1, 0))
    above = jnp.where(first + group < levels, 1.0, 0.0) * level(jnp.minimum(first + group, levels - 1))
    west = [ref[f, pl.ds(PAD - 1 + (first + j) * cells, cells), :] for j in range(group)]
    east = [ref[f, pl.ds(PAD + 1 + (first + j) * cells, cells), :] for j in range(group)]
    return [below] + [level(first + j) for j in range(group)] + [above], west, east


def beside(west, east, west_end, east_end):
    cells = west.shape[0]
    cell = iota(west.shape, 0)
    return jnp.where(cell == 0, west_end, west), jnp.where(cell == cells - 1, east_end, east)


def shares(wind):
    speed = 0.5 * COURANT * jnp.tanh(wind)
    return DIFFUSE_X - speed, DIFFUSE_X + speed


def vertical(value):
    levels = value.shape[0]
    level = iota(value.shape, 0)
    up = jnp.where(level < levels - 1, pltpu.roll(value, levels - 1, 0), 0.0)
    down = jnp.where(level > 0, pltpu.roll(value, 1, 0), 0.0)
    return up + down


def folded(value):
    total = value[0:8]
    for i in range(8, value.shape[0], 8):
        total = total + value[i : i + 8]
    return total


def over_rows(ref, f, levels):
    total = ref[f, pl.ds(0, levels, stride=8), :]
    for i in range(1, 8):
        total = total + ref[f, pl.ds(i, levels, stride=8), :]
    return total


def first_kernel(cells, _, left_ref, right_ref, state_ref, end_ref, fold_ref, done_ref, old_ref):
    fields, levels, _ = end_ref.shape[1:]
    group = 4

    def column(cell):
        return [state_ref[f, pl.ds(PAD + cell, levels, stride=cells), :] for f in range(fields)]

    ends = [column(cell) for cell in (0, cells - 1)]
    for side in range(2):
        for f in range(fields):
            end_ref[side, f] = ends[side][f]

    def level_at(k, rows=cells):
        return pl.ds(pl.multiple_of(PAD + k * cells, 8), rows)

    old_ref[...] = jnp.zeros(old_ref.shape, F32)

    @pl.loop(0, levels // group)
    def _(step):
        first = step * group
        stacks = [stack(state_ref, f, first, group, cells, levels) for f in range(fields)]
        for j in range(group):
            k = first + j
            from_east, from_west = shares(stacks[0][0][j + 1])
            moved = []
            for f in range(fields):
                down, centre, up = stacks[f][0][j : j + 3]
                if j == 0:
                    down = old_ref[f]
                west, east = beside(
                    stacks[f][1][j], stacks[f][2][j], left_ref[1, f, pl.ds(k, 1), :], right_ref[0, f, pl.ds(k, 1), :]
                )
                fold_ref[f, pl.ds(pl.multiple_of(k * 8, 8), 8), :] = folded(centre)
                moved.append(CENTRE * centre + DIFFUSE_Z * (up + down) + from_east * east + from_west * west)
            for f, value in enumerate(physics(moved)):
                done_ref[f, j * cells : (j + 1) * cells] = value
        for f in range(fields):
            old_ref[f] = state_ref[f, level_at(first + group - 1), :]
            state_ref[f, level_at(first, group * cells), :] = done_ref[f]

    def halo(west, centre, east, side):
        from_east, from_west = shares(centre[0])
        moved = [
            CENTRE * centre[f] + DIFFUSE_Z * vertical(centre[f]) + from_east * east[f] + from_west * west[f]
            for f in range(fields)
        ]
        for f, value in enumerate(physics(moved)):
            end_ref[side, f] = value

    own = [[end_ref[side, f] for f in range(fields)] for side in range(2)]
    halo(left_ref[0], left_ref[1], own[0], 0)
    halo(own[1], right_ref[0], right_ref[1], 1)
    for f in range(fields):
        end_ref[2, f] = over_rows(fold_ref, f, levels)


def second_kernel(
    force_ref, pre_ref, end_ref, out_ref, part_ref, rest_ref, push_ref, shift_ref, next_ref, fold_ref, sems
):
    fields, levels, _ = end_ref.shape[1:]
    cells = out_ref.shape[1] // levels
    blocks = force_ref.shape[0]
    share = levels // blocks
    group = 4
    for f in range(fields):
        for b in range(blocks):
            push_ref[f, b * share : (b + 1) * share] = force_ref[b, f * share : (f + 1) * share]
    for f in range(fields):
        push = push_ref[f]
        shift_ref[f] = (1.0 - 2.0 * DIFFUSE_Z) * push + DIFFUSE_Z * vertical(push)
    copies = []
    for b in range(blocks):

        @pl.loop(0, share // group)
        def _(step):
            first = b * share + step * group
            stacks = [stack(pre_ref, f, first, group, cells, levels) for f in range(fields)]
            for j in range(group):
                k = first + j
                push = [push_ref[f, pl.ds(k, 1), :] for f in range(fields)]
                from_east, from_west = shares(stacks[0][0][j + 1] + push[0])
                moved = []
                for f in range(fields):
                    down, centre, up = stacks[f][0][j : j + 3]
                    west, east = beside(
                        stacks[f][1][j], stacks[f][2][j], end_ref[0, f, pl.ds(k, 1), :], end_ref[1, f, pl.ds(k, 1), :]
                    )
                    moved.append(
                        (CENTRE * centre + shift_ref[f, pl.ds(k, 1), :])
                        + DIFFUSE_Z * (up + down)
                        + from_east * east
                        + from_west * west
                    )
                for f, value in enumerate(physics(moved)):
                    value = value + push[f]
                    if b < blocks - 1:
                        next_ref[f, pl.ds(pl.multiple_of(k * cells, 8), cells), :] = value
                    else:
                        rest_ref[f, pl.ds(pl.multiple_of((k - b * share) * cells, 8), cells), :] = value
                    fold_ref[f, pl.ds(pl.multiple_of(k * 8, 8), 8), :] = folded(value)

        if b == blocks - 1:
            break
        here = pl.ds(b * share * cells, share * cells)
        copy = pltpu.make_async_copy(next_ref.at[:, here], out_ref.at[:, here], sems.at[b])
        copy.start()
        copies.append(copy)
    for f in range(fields):
        change = over_rows(fold_ref, f, levels) - end_ref[2, f]
        for b in range(blocks):
            part_ref[b, f * share : (f + 1) * share] = change[b * share : (b + 1) * share]
    for copy in copies:
        copy.wait()


def back_kernel(scale, part_ref, slots_ref, out_ref):
    blocks, rows, lanes = part_ref.shape
    total = part_ref[0]
    for b in range(1, blocks):
        total = total + part_ref[b]
    slots = slots_ref[...]
    message = 0.0
    for term in thirds(total * scale):
        message = message + dot_nt(slots, jnp.concatenate([term, term], axis=0))
    owners = message.shape[0] // 2
    first = iota((owners, 2 * rows), 1) < rows
    out_ref[:, 0, :] = jnp.where(first, message[0:owners], message[owners:])


def final_kernel(got_ref, send_ref, smooth_ref, rest_ref, _, dyn_hbm, crm_hbm, dyn_ref, sems):
    rows, columns = smooth_ref.shape
    size = rest_ref.shape[1]
    rest = pltpu.make_async_copy(rest_ref, crm_hbm.at[:, pl.ds(crm_hbm.shape[1] - size, size)], sems.at[0])
    rest.start()
    got = got_ref[:, 0, :]
    got = jnp.concatenate([got[:, 0:rows], got[:, rows:]], axis=0)
    dyn_ref[...] = smooth_ref[...] + sum(dot_tn(term, send_ref[...]) for term in thirds(got))
    copy = pltpu.make_async_copy(dyn_ref, dyn_hbm, sems.at[1])
    copy.start()
    rest.wait()
    copy.wait()


def call(kernel, outs, *args, scalars=(), far=(), scratch=(), same=None, cost=0, limit=4, name=None):
    vmem = pl.BlockSpec(memory_space=pltpu.VMEM)
    smem = pl.BlockSpec(memory_space=pltpu.SMEM)
    hbm = pl.BlockSpec(memory_space=pltpu.HBM)
    args = [pltpu.with_memory_space_constraint(a, pltpu.HBM) if i in far else a for i, a in enumerate(args)]
    return pl.pallas_call(
        kernel,
        out_shape=[s for s, _ in outs],
        in_specs=[smem if i in scalars else hbm if i in far else vmem for i in range(len(args))],
        out_specs=[hbm if distant else vmem for _, distant in outs],
        scratch_shapes=list(scratch),
        input_output_aliases=same or {},
        cost_estimate=pl.CostEstimate(flops=cost, bytes_accessed=0, transcendentals=0) if cost else None,
        compiler_params=pltpu.CompilerParams(vmem_limit_bytes=limit * 1024 * 1024),
        name=name,
    )(*args)


def near(*shape, dtype=F32):
    return (jax.ShapeDtypeStruct(shape, dtype), False)


def there(*shape, dtype=F32):
    return (pltpu.HBM(shape, dtype), True)


def per_device(crm_state, dyn_state, ls_tend, span_slot, neighbours):
    elem_count = lax.axis_size("elem")
    lev_count = lax.axis_size("lev")
    fields, share, columns = dyn_state.shape
    _, levels, cells, _ = crm_state.shape
    rows = fields * share
    dyn = dyn_state.reshape(rows, columns)
    tend = ls_tend.reshape(rows, columns)
    slot = span_slot.reshape(1, columns)
    crm_flat = crm_state.reshape(fields, levels * cells, columns)
    dma = pltpu.SemaphoreType.DMA

    core_pairs = [(i, i ^ 1) for i in range(elem_count)]
    chip_pairs = [(i, ((i ^ 1) + (2 if i & 1 else -2)) % elem_count) for i in range(elem_count)]
    from_chip = lax.ppermute(dyn, "elem", chip_pairs)

    odd = (lax.axis_index("elem") & 1).astype(jnp.int32).reshape(1, 1)
    square = near(columns, columns, dtype=BF16)
    padded = (fields, levels * cells + 2 * PAD, columns)
    edge = (2, fields, levels, columns)
    mself, mchip, mcore, send, dyn_near, tend_near, slot_near = call(
        maps_kernel,
        [
            square,
            square,
            square,
            near(2 * elem_count, columns, dtype=BF16),
            near(rows, columns),
            near(rows, columns),
            near(1, columns, dtype=jnp.int32),
        ],
        odd,
        neighbours.T,
        slot,
        dyn,
        tend,
        scalars=(0,),
        far=(1, 2, 3, 4),
        scratch=[pltpu.VMEM((4, columns // 4), jnp.int32), dma((4,))],
        cost=10**10,
        name="maps",
    )
    from_core = lax.ppermute(dyn_near, "elem", core_pairs)
    state, left, right = call(
        functools.partial(state_kernel, cells),
        [near(*padded), there(*edge), there(*edge)],
        crm_flat,
        scratch=[pltpu.VMEM(edge, F32), pltpu.VMEM(edge, F32), dma((2,))],
        name="state",
    )
    message, smoothed = call(
        forcing_kernel,
        [there(elem_count, 2, columns), near(rows, columns)],
        from_core,
        from_chip,
        dyn_near,
        tend_near,
        slot_near,
        mself,
        mchip,
        mcore,
        send,
        left,
        far=(9,),
        scratch=[pltpu.VMEM((elem_count, 2, columns), F32), dma((2,))],
        name="forcing",
    )
    got = lax.all_to_all(message, "elem", split_axis=0, concat_axis=0, tiled=True)

    ring = [(i, (i + 1) % lev_count) for i in range(lev_count)]
    from_left = lax.ppermute(right, "lev", ring)
    from_right = lax.ppermute(left, "lev", [(j, i) for i, j in ring])
    eighths = (fields, levels * 8, columns)
    pre, ends = call(
        functools.partial(first_kernel, cells),
        [near(*padded), near(3, fields, levels, columns)],
        state,
        from_left,
        from_right,
        scratch=[
            pltpu.VMEM(eighths, F32),
            pltpu.VMEM((fields, 4 * cells, columns), F32),
            pltpu.VMEM((fields, cells, columns), F32),
        ],
        same={0: 0},
        limit=8,
        name="first_substep",
    )

    placed, slots = call(
        place_kernel,
        [there(lev_count, rows, columns), near(2 * elem_count, columns, dtype=BF16)],
        got,
        scratch=[pltpu.VMEM((rows, columns), F32), dma((lev_count,))],
        name="place",
    )
    force = lax.all_to_all(placed, "lev", split_axis=0, concat_axis=0, tiled=True)
    size = levels // lev_count * cells
    crm_next, parts, rest = call(
        second_kernel,
        [there(fields, levels * cells, columns), near(lev_count, rows, columns), near(fields, size, columns)],
        force,
        pre,
        ends,
        scratch=[
            pltpu.VMEM((fields, levels, columns), F32),
            pltpu.VMEM((fields, levels, columns), F32),
            pltpu.VMEM((fields, levels * cells - size, columns), F32),
            pltpu.VMEM(eighths, F32),
            dma((lev_count - 1,)),
        ],
        limit=8,
        name="second_substep",
    )
    parts = lax.all_to_all(parts, "lev", split_axis=0, concat_axis=0, tiled=True)
    scale = 1.0 / (cells * lev_count * SUBSTEPS)
    (answer,) = call(
        functools.partial(back_kernel, scale),
        [near(elem_count, 1, 2 * rows)],
        parts,
        slots,
        name="back",
    )
    back = lax.all_to_all(answer, "elem", split_axis=0, concat_axis=0, tiled=True)
    dynamics, crm_next = call(
        final_kernel,
        [there(rows, columns), there(fields, levels * cells, columns)],
        back,
        send,
        smoothed,
        rest,
        crm_next,
        far=(4,),
        scratch=[pltpu.VMEM((rows, columns), F32), dma((2,))],
        same={4: 1},
        name="final",
    )
    return crm_next.reshape(crm_state.shape), dynamics.reshape(fields, share, columns)


def solution(mesh):
    return jax.shard_map(
        per_device,
        mesh=mesh,
        in_specs=(
            P(None, None, "lev", "elem"),
            P(None, "lev", "elem"),
            P(None, "lev", "elem"),
            P("elem"),
            P("elem", None),
        ),
        out_specs=(P(None, None, "lev", "elem"), P(None, "lev", "elem")),
        check_vma=False,
    )
```

```python
import functools

import jax
import jax.numpy as jnp
from jax import lax
from jax.experimental import pallas as pl
from jax.experimental.pallas import tpu as pltpu
from jax.sharding import PartitionSpec as P

SUBSTEPS = 2
SAT_ITERS = 3
DIFFUSE_X = 0.2
DIFFUSE_Z = 0.1
COURANT = 0.3
SAT_SLOPE = 0.3
LOG2_E = 1.4426950408889634
LATENT = 0.5
RELAX_RATE = 0.5
AUTOCONV = 0.2
BUOYANCY = 0.5
EDGE_WEIGHT = 0.25
CENTRE = 1.0 - 2.0 * DIFFUSE_X - 2.0 * DIFFUSE_Z

FIRST = 72
FIRST_BACK = 72

PAD = 8

F32 = jnp.float32
BF16 = jnp.bfloat16


def iota(shape, dim):
    return lax.broadcasted_iota(jnp.int32, shape, dim)


def thirds(x):
    high = x.astype(BF16)
    rest = x - high.astype(F32)
    middle = rest.astype(BF16)
    low = (rest - middle.astype(F32)).astype(BF16)
    return high, middle, low


def dot(a, b):
    return lax.dot_general(a, b, (((1,), (0,)), ((), ())), preferred_element_type=F32)


def dot_nt(a, b):
    return lax.dot_general(a, b, (((1,), (1,)), ((), ())), preferred_element_type=F32)


def dot_tn(a, b):
    return lax.dot_general(a, b, (((0,), (0,)), ((), ())), preferred_element_type=F32)


def physics(fields):
    wind_u, wind_w, temper, vapour, cloud_liq, cloud_ice, rain_water, snow_water = fields
    temper_start = temper
    for _ in range(SAT_ITERS):
        saturated = jnp.exp2(SAT_SLOPE * LOG2_E * temper)
        change = RELAX_RATE * (vapour - saturated) / (1.0 + LATENT * SAT_SLOPE * saturated)
        change = jnp.maximum(change, -cloud_liq)
        cloud_liq = cloud_liq + change
        vapour = vapour - change
        temper = temper + LATENT * change
    rainout = AUTOCONV * jnp.maximum(cloud_liq, 0.0)
    snowout = AUTOCONV * jnp.maximum(cloud_ice, 0.0)
    return [
        wind_u,
        wind_w + BUOYANCY * (temper - temper_start),
        temper,
        vapour,
        cloud_liq - rainout,
        cloud_ice - snowout,
        rain_water + rainout,
        snow_water + snowout,
    ]


def maps(odd_ref, nb_ref, slot_ref, self_ref, chip_ref, core_ref, send_ref):
    column_count = slot_ref.shape[1]
    elem_local = column_count // 4
    shape = (column_count, column_count)
    row, col = iota(shape, 0), iota(shape, 1)
    row_corner, col_corner = row & 3, col & 3
    spread = (iota((elem_local, column_count), 1) // 4 == iota((elem_local, column_count), 0)).astype(BF16)
    code = nb_ref[...]
    high = dot((code >> 7).astype(F32).astype(BF16), spread)
    low = dot((code & 127).astype(F32).astype(BF16), spread)
    code = (high * 128.0 + low).astype(jnp.int32)
    corner = iota((1, column_count), 1) & 3
    along_y = jnp.where(corner < 2, code[0:1], code[2:3])
    along_x = jnp.where((corner & 1) == 1, code[1:2], code[3:4])

    def partner(which):
        edge = which & 3
        place = (which >> 2) % elem_local
        touches = jnp.where(
            edge == 0,
            (row_corner < 2).astype(F32),
            jnp.where(
                edge == 1,
                (row_corner & 1).astype(F32),
                jnp.where(edge == 2, (row_corner >= 2).astype(F32), 1.0 - (row_corner & 1).astype(F32)),
            ),
        )
        return jnp.where((row >> 2) == place, touches, 0.0)

    weight = 0.5 * EDGE_WEIGHT
    own = ((row_corner >> 1) == (col_corner >> 1)).astype(F32) + ((row_corner & 1) == (col_corner & 1)).astype(F32)
    own = jnp.where((row >> 2) == (col >> 2), own, 0.0)
    self_ref[...] = (weight * (partner(along_y) - own)).astype(BF16)
    beside = weight * partner(along_x)
    from_core = (col_corner & 1) != odd_ref[0, 0]
    core_ref[...] = jnp.where(from_core, beside, 0.0).astype(BF16)
    chip_ref[...] = jnp.where(from_core, 0.0, beside).astype(BF16)

    spans = send_ref.shape[0] // 2
    goes = row == (slot_ref[...] // column_count + (spans - FIRST)) % spans
    onehot = goes.astype(F32).astype(BF16)
    rank = jnp.sum(jnp.where(row < col, dot_tn(onehot, onehot), 0.0), axis=0, keepdims=True)
    send_ref[0:column_count] = jnp.where(rank < 0.5, goes.astype(F32), 0.0).astype(BF16)
    send_ref[column_count:] = jnp.where(rank > 0.5, goes.astype(F32), 0.0).astype(BF16)


def forcing_kernel(
    core_ref, chip_ref, dyn_ref, ls_ref, slot_ref, mself, mchip, mcore, send_ref, _, out_hbm, smooth_ref, out_ref, sems
):
    rows, column_count = dyn_ref.shape
    dyn = dyn_ref[...]

    def through(value, matrix):
        return dot(jnp.concatenate(thirds(value), axis=0), matrix[...])

    change = through(dyn, mself) + through(core_ref[...], mcore) + through(chip_ref[...], mchip)
    change = change[0:rows] + change[rows : 2 * rows] + change[2 * rows :]
    smooth_ref[...] = dyn + change
    slot = ((slot_ref[...] % column_count) + 1).astype(F32)
    rest = column_count - rows
    extra = jnp.where(iota((rest, column_count), 0) == 0, slot, 0.0).astype(BF16)
    empty = jnp.zeros((rest, column_count), BF16)
    high, middle, low = thirds(ls_ref[...] + change)
    terms = [
        jnp.concatenate([high, extra], axis=0),
        jnp.concatenate([middle, empty], axis=0),
        jnp.concatenate([low, empty], axis=0),
    ]
    spans = send_ref.shape[0] // 2
    parts = sems.shape[0]
    size = spans // parts
    copies = []
    for part in range(parts):
        here = slice(part * size, (part + 1) * size)
        send = jnp.concatenate([send_ref[here], send_ref[spans + here.start : spans + here.stop]], axis=0)
        message = dot_nt(send, terms[0]) + dot_nt(send, terms[1]) + dot_nt(send, terms[2])
        out_ref[here, 0, :] = message[0:size]
        out_ref[here, 1, :] = message[size:]
        copies.append(pltpu.make_async_copy(out_ref.at[here], out_hbm.at[here], sems.at[part]))
        copies[part].start()
    for copy in copies:
        copy.wait()


def place_kernel(got_ref, out_hbm, slots_ref, placed_ref, sems):
    count, rows, column_count = out_hbm.shape
    got = jnp.concatenate([got_ref[:, 0, :], got_ref[:, 1, :]], axis=0)
    slot = got[:, rows : rows + 1] - 1.0
    lanes = iota((got.shape[0], column_count), 1).astype(F32)
    slots = (lanes == slot).astype(F32).astype(BF16)
    slots_ref[...] = slots
    placed_ref[...] = sum(dot_tn(term, slots) for term in thirds(got[:, 0:rows]))
    copies = [pltpu.make_async_copy(placed_ref, out_hbm.at[i], sems.at[i]) for i in range(count)]
    for copy in copies:
        copy.start()
    for copy in copies:
        copy.wait()


def maps_kernel(
    odd_ref, nb_hbm, slot_hbm, dyn_hbm, tend_hbm,
    self_ref, chip_ref, core_ref, send_ref, dyn_ref, tend_ref, slot_ref, nb_ref, sems,
):
    pairs = [(slot_hbm, slot_ref), (nb_hbm, nb_ref), (dyn_hbm, dyn_ref), (tend_hbm, tend_ref)]
    copies = [pltpu.make_async_copy(source, target, sems.at[i]) for i, (source, target) in enumerate(pairs)]
    for copy in copies:
        copy.start()
    copies[0].wait()
    copies[1].wait()
    maps(odd_ref, nb_ref, slot_ref, self_ref, chip_ref, core_ref, send_ref)
    for copy in copies[2:]:
        copy.wait()


def state_kernel(cells, whole_ref, crm_ref, left_hbm, right_hbm, left_ref, right_ref, sems):
    fields, size, _ = whole_ref.shape
    levels = left_ref.shape[2]
    for f in range(fields):
        for j in range(2):
            left_ref[j, f] = whole_ref[f, pl.ds(j, levels, stride=cells), :]
            right_ref[j, f] = whole_ref[f, pl.ds(cells - 2 + j, levels, stride=cells), :]
    copies = []
    for i, (near, far) in enumerate(((left_ref, left_hbm), (right_ref, right_hbm))):
        copies.append(pltpu.make_async_copy(near, far, sems.at[i]))
        copies[i].start()
    step = 64

    @pl.loop(0, size // step)
    def _(i):
        for f in range(fields):
            source = pl.ds(pl.multiple_of(i * step, 8), step)
            crm_ref[f, pl.ds(pl.multiple_of(PAD + i * step, 8), step), :] = whole_ref[f, source, :]

    for copy in copies:
        copy.wait()


def stack(ref, f, first, group, cells, levels):
    def level(k):
        return ref[f, pl.ds(pl.multiple_of(PAD + k * cells, 8), cells), :]

    below = jnp.where(first > 0, 1.0, 0.0) * level(jnp.maximum(first - 1, 0))
    above = jnp.where(first + group < levels, 1.0, 0.0) * level(jnp.minimum(first + group, levels - 1))
    west = [ref[f, pl.ds(PAD - 1 + (first + j) * cells, cells), :] for j in range(group)]
    east = [ref[f, pl.ds(PAD + 1 + (first + j) * cells, cells), :] for j in range(group)]
    return [below] + [level(first + j) for j in range(group)] + [above], west, east


def beside(west, east, west_end, east_end):
    cells = west.shape[0]
    cell = iota(west.shape, 0)
    return jnp.where(cell == 0, west_end, west), jnp.where(cell == cells - 1, east_end, east)


def shares(wind):
    speed = 0.5 * COURANT * jnp.tanh(wind)
    return DIFFUSE_X - speed, DIFFUSE_X + speed


def vertical(value):
    levels = value.shape[0]
    level = iota(value.shape, 0)
    up = jnp.where(level < levels - 1, pltpu.roll(value, levels - 1, 0), 0.0)
    down = jnp.where(level > 0, pltpu.roll(value, 1, 0), 0.0)
    return up + down


def folded(value):
    total = value[0:8]
    for i in range(8, value.shape[0], 8):
        total = total + value[i : i + 8]
    return total


def over_rows(ref, f, levels):
    total = ref[f, pl.ds(0, levels, stride=8), :]
    for i in range(1, 8):
        total = total + ref[f, pl.ds(i, levels, stride=8), :]
    return total


def first_kernel(cells, _, left_ref, right_ref, state_ref, end_ref, fold_ref, done_ref, old_ref):
    fields, levels, _ = end_ref.shape[1:]
    group = 4

    def column(cell):
        return [state_ref[f, pl.ds(PAD + cell, levels, stride=cells), :] for f in range(fields)]

    ends = [column(cell) for cell in (0, cells - 1)]
    for side in range(2):
        for f in range(fields):
            end_ref[side, f] = ends[side][f]

    def level_at(k, rows=cells):
        return pl.ds(pl.multiple_of(PAD + k * cells, 8), rows)

    old_ref[...] = jnp.zeros(old_ref.shape, F32)

    @pl.loop(0, levels // group)
    def _(step):
        first = step * group
        stacks = [stack(state_ref, f, first, group, cells, levels) for f in range(fields)]
        for j in range(group):
            k = first + j
            from_east, from_west = shares(stacks[0][0][j + 1])
            moved = []
            for f in range(fields):
                down, centre, up = stacks[f][0][j : j + 3]
                if j == 0:
                    down = old_ref[f]
                west, east = beside(
                    stacks[f][1][j], stacks[f][2][j], left_ref[1, f, pl.ds(k, 1), :], right_ref[0, f, pl.ds(k, 1), :]
                )
                fold_ref[f, pl.ds(pl.multiple_of(k * 8, 8), 8), :] = folded(centre)
                moved.append(CENTRE * centre + DIFFUSE_Z * (up + down) + from_east * east + from_west * west)
            for f, value in enumerate(physics(moved)):
                done_ref[f, j * cells : (j + 1) * cells] = value
        for f in range(fields):
            old_ref[f] = state_ref[f, level_at(first + group - 1), :]
            state_ref[f, level_at(first, group * cells), :] = done_ref[f]

    def halo(west, centre, east, side):
        from_east, from_west = shares(centre[0])
        moved = [
            CENTRE * centre[f] + DIFFUSE_Z * vertical(centre[f]) + from_east * east[f] + from_west * west[f]
            for f in range(fields)
        ]
        for f, value in enumerate(physics(moved)):
            end_ref[side, f] = value

    own = [[end_ref[side, f] for f in range(fields)] for side in range(2)]
    halo(left_ref[0], left_ref[1], own[0], 0)
    halo(own[1], right_ref[0], right_ref[1], 1)
    for f in range(fields):
        end_ref[2, f] = over_rows(fold_ref, f, levels)


def second_kernel(
    force_ref, pre_ref, end_ref, out_ref, part_ref, rest_ref, push_ref, shift_ref, next_ref, fold_ref, sems
):
    fields, levels, _ = end_ref.shape[1:]
    cells = out_ref.shape[1] // levels
    blocks = force_ref.shape[0]
    share = levels // blocks
    group = 4
    for f in range(fields):
        for b in range(blocks):
            push_ref[f, b * share : (b + 1) * share] = force_ref[b, f * share : (f + 1) * share]
    for f in range(fields):
        push = push_ref[f]
        shift_ref[f] = (1.0 - 2.0 * DIFFUSE_Z) * push + DIFFUSE_Z * vertical(push)
    copies = []
    for b in range(blocks):

        @pl.loop(0, share // group)
        def _(step):
            first = b * share + step * group
            stacks = [stack(pre_ref, f, first, group, cells, levels) for f in range(fields)]
            for j in range(group):
                k = first + j
                push = [push_ref[f, pl.ds(k, 1), :] for f in range(fields)]
                from_east, from_west = shares(stacks[0][0][j + 1] + push[0])
                moved = []
                for f in range(fields):
                    down, centre, up = stacks[f][0][j : j + 3]
                    west, east = beside(
                        stacks[f][1][j], stacks[f][2][j], end_ref[0, f, pl.ds(k, 1), :], end_ref[1, f, pl.ds(k, 1), :]
                    )
                    moved.append(
                        (CENTRE * centre + shift_ref[f, pl.ds(k, 1), :])
                        + DIFFUSE_Z * (up + down)
                        + from_east * east
                        + from_west * west
                    )
                for f, value in enumerate(physics(moved)):
                    value = value + push[f]
                    if b < blocks - 1:
                        next_ref[f, pl.ds(pl.multiple_of(k * cells, 8), cells), :] = value
                    else:
                        rest_ref[f, pl.ds(pl.multiple_of((k - b * share) * cells, 8), cells), :] = value
                    fold_ref[f, pl.ds(pl.multiple_of(k * 8, 8), 8), :] = folded(value)

        if b == blocks - 1:
            break
        here = pl.ds(b * share * cells, share * cells)
        copy = pltpu.make_async_copy(next_ref.at[:, here], out_ref.at[:, here], sems.at[b])
        copy.start()
        copies.append(copy)
    for f in range(fields):
        change = over_rows(fold_ref, f, levels) - end_ref[2, f]
        for b in range(blocks):
            part_ref[b, f * share : (f + 1) * share] = change[b * share : (b + 1) * share]
    for copy in copies:
        copy.wait()


def back_kernel(scale, part_ref, slots_ref, out_ref):
    blocks, rows, lanes = part_ref.shape
    total = part_ref[0]
    for b in range(1, blocks):
        total = total + part_ref[b]
    slots = slots_ref[...]
    message = 0.0
    for term in thirds(total * scale):
        message = message + dot_nt(slots, jnp.concatenate([term, term], axis=0))
    owners = message.shape[0] // 2
    first = iota((owners, 2 * rows), 1) < rows
    message = jnp.where(first, message[0:owners], message[owners:])
    turn = (FIRST - FIRST_BACK) % owners
    out_ref[turn:, 0, :] = message[0 : owners - turn]
    if turn > 0:
        out_ref[0:turn, 0, :] = message[owners - turn :]


def final_kernel(got_ref, send_ref, smooth_ref, rest_ref, _, dyn_hbm, crm_hbm, dyn_ref, sems):
    rows, columns = smooth_ref.shape
    size = rest_ref.shape[1]
    rest = pltpu.make_async_copy(rest_ref, crm_hbm.at[:, pl.ds(crm_hbm.shape[1] - size, size)], sems.at[0])
    rest.start()
    turn = (FIRST - FIRST_BACK) % got_ref.shape[0]
    got = got_ref[turn:, 0, :]
    if turn > 0:
        got = jnp.concatenate([got, got_ref[0:turn, 0, :]], axis=0)
    got = jnp.concatenate([got[:, 0:rows], got[:, rows:]], axis=0)
    dyn_ref[...] = smooth_ref[...] + sum(dot_tn(term, send_ref[...]) for term in thirds(got))
    copy = pltpu.make_async_copy(dyn_ref, dyn_hbm, sems.at[1])
    copy.start()
    rest.wait()
    copy.wait()


def call(kernel, outs, *args, scalars=(), far=(), scratch=(), same=None, cost=0, limit=4, name=None):
    vmem = pl.BlockSpec(memory_space=pltpu.VMEM)
    smem = pl.BlockSpec(memory_space=pltpu.SMEM)
    hbm = pl.BlockSpec(memory_space=pltpu.HBM)
    args = [pltpu.with_memory_space_constraint(a, pltpu.HBM) if i in far else a for i, a in enumerate(args)]
    return pl.pallas_call(
        kernel,
        out_shape=[s for s, _ in outs],
        in_specs=[smem if i in scalars else hbm if i in far else vmem for i in range(len(args))],
        out_specs=[hbm if distant else vmem for _, distant in outs],
        scratch_shapes=list(scratch),
        input_output_aliases=same or {},
        cost_estimate=pl.CostEstimate(flops=cost, bytes_accessed=0, transcendentals=0) if cost else None,
        compiler_params=pltpu.CompilerParams(vmem_limit_bytes=limit * 1024 * 1024),
        name=name,
    )(*args)


def near(*shape, dtype=F32):
    return (jax.ShapeDtypeStruct(shape, dtype), False)


def there(*shape, dtype=F32):
    return (pltpu.HBM(shape, dtype), True)


def per_device(crm_state, dyn_state, ls_tend, span_slot, neighbours):
    elem_count = lax.axis_size("elem")
    lev_count = lax.axis_size("lev")
    fields, share, columns = dyn_state.shape
    _, levels, cells, _ = crm_state.shape
    rows = fields * share
    dyn = dyn_state.reshape(rows, columns)
    tend = ls_tend.reshape(rows, columns)
    slot = span_slot.reshape(1, columns)
    crm_flat = crm_state.reshape(fields, levels * cells, columns)
    dma = pltpu.SemaphoreType.DMA

    core_pairs = [(i, i ^ 1) for i in range(elem_count)]
    chip_pairs = [(i, ((i ^ 1) + (2 if i & 1 else -2)) % elem_count) for i in range(elem_count)]
    from_chip = lax.ppermute(dyn, "elem", chip_pairs)

    odd = (lax.axis_index("elem") & 1).astype(jnp.int32).reshape(1, 1)
    square = near(columns, columns, dtype=BF16)
    padded = (fields, levels * cells + 2 * PAD, columns)
    edge = (2, fields, levels, columns)
    mself, mchip, mcore, send, dyn_near, tend_near, slot_near = call(
        maps_kernel,
        [
            square,
            square,
            square,
            near(2 * elem_count, columns, dtype=BF16),
            near(rows, columns),
            near(rows, columns),
            near(1, columns, dtype=jnp.int32),
        ],
        odd,
        neighbours.T,
        slot,
        dyn,
        tend,
        scalars=(0,),
        far=(1, 2, 3, 4),
        scratch=[pltpu.VMEM((4, columns // 4), jnp.int32), dma((4,))],
        cost=10**10,
        name="maps",
    )
    from_core = lax.ppermute(dyn_near, "elem", core_pairs)
    state, left, right = call(
        functools.partial(state_kernel, cells),
        [near(*padded), there(*edge), there(*edge)],
        crm_flat,
        scratch=[pltpu.VMEM(edge, F32), pltpu.VMEM(edge, F32), dma((2,))],
        name="state",
    )
    message, smoothed = call(
        forcing_kernel,
        [there(elem_count, 2, columns), near(rows, columns)],
        from_core,
        from_chip,
        dyn_near,
        tend_near,
        slot_near,
        mself,
        mchip,
        mcore,
        send,
        left,
        far=(9,),
        scratch=[pltpu.VMEM((elem_count, 2, columns), F32), dma((2,))],
        name="forcing",
    )
    order, order_back = [[[(first + i) % elem_count for i in range(elem_count)]] for first in (FIRST, FIRST_BACK)]
    got = lax.all_to_all(message, "elem", split_axis=0, concat_axis=0, axis_index_groups=order, tiled=True)

    ring = [(i, (i + 1) % lev_count) for i in range(lev_count)]
    from_left = lax.ppermute(right, "lev", ring)
    from_right = lax.ppermute(left, "lev", [(j, i) for i, j in ring])
    eighths = (fields, levels * 8, columns)
    pre, ends = call(
        functools.partial(first_kernel, cells),
        [near(*padded), near(3, fields, levels, columns)],
        state,
        from_left,
        from_right,
        scratch=[
            pltpu.VMEM(eighths, F32),
            pltpu.VMEM((fields, 4 * cells, columns), F32),
            pltpu.VMEM((fields, cells, columns), F32),
        ],
        same={0: 0},
        limit=8,
        name="first_substep",
    )

    placed, slots = call(
        place_kernel,
        [there(lev_count, rows, columns), near(2 * elem_count, columns, dtype=BF16)],
        got,
        scratch=[pltpu.VMEM((rows, columns), F32), dma((lev_count,))],
        name="place",
    )
    force = lax.all_to_all(placed, "lev", split_axis=0, concat_axis=0, tiled=True)
    size = levels // lev_count * cells
    crm_next, parts, rest = call(
        second_kernel,
        [there(fields, levels * cells, columns), near(lev_count, rows, columns), near(fields, size, columns)],
        force,
        pre,
        ends,
        scratch=[
            pltpu.VMEM((fields, levels, columns), F32),
            pltpu.VMEM((fields, levels, columns), F32),
            pltpu.VMEM((fields, levels * cells - size, columns), F32),
            pltpu.VMEM(eighths, F32),
            dma((lev_count - 1,)),
        ],
        limit=8,
        name="second_substep",
    )
    parts = lax.all_to_all(parts, "lev", split_axis=0, concat_axis=0, tiled=True)
    scale = 1.0 / (cells * lev_count * SUBSTEPS)
    (answer,) = call(
        functools.partial(back_kernel, scale),
        [near(elem_count, 1, 2 * rows)],
        parts,
        slots,
        name="back",
    )
    back = lax.all_to_all(answer, "elem", split_axis=0, concat_axis=0, axis_index_groups=order_back, tiled=True)
    dynamics, crm_next = call(
        final_kernel,
        [there(rows, columns), there(fields, levels * cells, columns)],
        back,
        send,
        smoothed,
        rest,
        crm_next,
        far=(4,),
        scratch=[pltpu.VMEM((rows, columns), F32), dma((2,))],
        same={4: 1},
        name="final",
    )
    return crm_next.reshape(crm_state.shape), dynamics.reshape(fields, share, columns)


def solution(mesh):
    return jax.shard_map(
        per_device,
        mesh=mesh,
        in_specs=(
            P(None, None, "lev", "elem"),
            P(None, "lev", "elem"),
            P(None, "lev", "elem"),
            P("elem"),
            P("elem", None),
        ),
        out_specs=(P(None, None, "lev", "elem"), P(None, "lev", "elem")),
        check_vma=False,
    )
```

```python
import functools

import jax
import jax.numpy as jnp
from jax import lax
from jax.experimental import pallas as pl
from jax.experimental.pallas import tpu as pltpu
from jax.sharding import PartitionSpec as P

SUBSTEPS = 2
SAT_ITERS = 3
DIFFUSE_X = 0.2
DIFFUSE_Z = 0.1
COURANT = 0.3
SAT_SLOPE = 0.3
LOG2_E = 1.4426950408889634
LATENT = 0.5
RELAX_RATE = 0.5
AUTOCONV = 0.2
BUOYANCY = 0.5
EDGE_WEIGHT = 0.25
CENTRE = 1.0 - 2.0 * DIFFUSE_X - 2.0 * DIFFUSE_Z

FIRST = 96
FIRST_BACK = 72

PAD = 8

F32 = jnp.float32
BF16 = jnp.bfloat16


def iota(shape, dim):
    return lax.broadcasted_iota(jnp.int32, shape, dim)


def thirds(x):
    high = x.astype(BF16)
    rest = x - high.astype(F32)
    middle = rest.astype(BF16)
    low = (rest - middle.astype(F32)).astype(BF16)
    return high, middle, low


def dot(a, b):
    return lax.dot_general(a, b, (((1,), (0,)), ((), ())), preferred_element_type=F32)


def dot_nt(a, b):
    return lax.dot_general(a, b, (((1,), (1,)), ((), ())), preferred_element_type=F32)


def dot_tn(a, b):
    return lax.dot_general(a, b, (((0,), (0,)), ((), ())), preferred_element_type=F32)


def physics(fields):
    wind_u, wind_w, temper, vapour, cloud_liq, cloud_ice, rain_water, snow_water = fields
    temper_start = temper
    for _ in range(SAT_ITERS):
        saturated = jnp.exp2(SAT_SLOPE * LOG2_E * temper)
        change = RELAX_RATE * (vapour - saturated) / (1.0 + LATENT * SAT_SLOPE * saturated)
        change = jnp.maximum(change, -cloud_liq)
        cloud_liq = cloud_liq + change
        vapour = vapour - change
        temper = temper + LATENT * change
    rainout = AUTOCONV * jnp.maximum(cloud_liq, 0.0)
    snowout = AUTOCONV * jnp.maximum(cloud_ice, 0.0)
    return [
        wind_u,
        wind_w + BUOYANCY * (temper - temper_start),
        temper,
        vapour,
        cloud_liq - rainout,
        cloud_ice - snowout,
        rain_water + rainout,
        snow_water + snowout,
    ]


def maps(odd_ref, nb_ref, slot_ref, self_ref, chip_ref, core_ref, send_ref):
    column_count = slot_ref.shape[1]
    elem_local = column_count // 4
    shape = (column_count, column_count)
    row, col = iota(shape, 0), iota(shape, 1)
    row_corner, col_corner = row & 3, col & 3
    spread = (iota((elem_local, column_count), 1) // 4 == iota((elem_local, column_count), 0)).astype(BF16)
    code = nb_ref[...]
    high = dot((code >> 7).astype(F32).astype(BF16), spread)
    low = dot((code & 127).astype(F32).astype(BF16), spread)
    code = (high * 128.0 + low).astype(jnp.int32)
    corner = iota((1, column_count), 1) & 3
    along_y = jnp.where(corner < 2, code[0:1], code[2:3])
    along_x = jnp.where((corner & 1) == 1, code[1:2], code[3:4])

    def partner(which):
        edge = which & 3
        place = (which >> 2) % elem_local
        touches = jnp.where(
            edge == 0,
            (row_corner < 2).astype(F32),
            jnp.where(
                edge == 1,
                (row_corner & 1).astype(F32),
                jnp.where(edge == 2, (row_corner >= 2).astype(F32), 1.0 - (row_corner & 1).astype(F32)),
            ),
        )
        return jnp.where((row >> 2) == place, touches, 0.0)

    weight = 0.5 * EDGE_WEIGHT
    own = ((row_corner >> 1) == (col_corner >> 1)).astype(F32) + ((row_corner & 1) == (col_corner & 1)).astype(F32)
    own = jnp.where((row >> 2) == (col >> 2), own, 0.0)
    self_ref[...] = (weight * (partner(along_y) - own)).astype(BF16)
    beside = weight * partner(along_x)
    from_core = (col_corner & 1) != odd_ref[0, 0]
    core_ref[...] = jnp.where(from_core, beside, 0.0).astype(BF16)
    chip_ref[...] = jnp.where(from_core, 0.0, beside).astype(BF16)

    spans = send_ref.shape[0] // 2
    goes = row == (slot_ref[...] // column_count + (spans - FIRST)) % spans
    onehot = goes.astype(F32).astype(BF16)
    rank = jnp.sum(jnp.where(row < col, dot_tn(onehot, onehot), 0.0), axis=0, keepdims=True)
    send_ref[0:column_count] = jnp.where(rank < 0.5, goes.astype(F32), 0.0).astype(BF16)
    send_ref[column_count:] = jnp.where(rank > 0.5, goes.astype(F32), 0.0).astype(BF16)


def forcing_kernel(
    core_ref, chip_ref, dyn_ref, ls_ref, slot_ref, mself, mchip, mcore, send_ref, _, out_hbm, smooth_ref, out_ref, sems
):
    rows, column_count = dyn_ref.shape
    dyn = dyn_ref[...]

    def through(value, matrix):
        return dot(jnp.concatenate(thirds(value), axis=0), matrix[...])

    change = through(dyn, mself) + through(core_ref[...], mcore) + through(chip_ref[...], mchip)
    change = change[0:rows] + change[rows : 2 * rows] + change[2 * rows :]
    smooth_ref[...] = dyn + change
    slot = ((slot_ref[...] % column_count) + 1).astype(F32)
    rest = column_count - rows
    extra = jnp.where(iota((rest, column_count), 0) == 0, slot, 0.0).astype(BF16)
    empty = jnp.zeros((rest, column_count), BF16)
    high, middle, low = thirds(ls_ref[...] + change)
    terms = [
        jnp.concatenate([high, extra], axis=0),
        jnp.concatenate([middle, empty], axis=0),
        jnp.concatenate([low, empty], axis=0),
    ]
    spans = send_ref.shape[0] // 2
    parts = sems.shape[0]
    size = spans // parts
    copies = []
    for part in range(parts):
        here = slice(part * size, (part + 1) * size)
        send = jnp.concatenate([send_ref[here], send_ref[spans + here.start : spans + here.stop]], axis=0)
        message = dot_nt(send, terms[0]) + dot_nt(send, terms[1]) + dot_nt(send, terms[2])
        out_ref[here, 0, :] = message[0:size]
        out_ref[here, 1, :] = message[size:]
        copies.append(pltpu.make_async_copy(out_ref.at[here], out_hbm.at[here], sems.at[part]))
        copies[part].start()
    for copy in copies:
        copy.wait()


def place_kernel(got_ref, out_hbm, slots_ref, placed_ref, sems):
    count, rows, column_count = out_hbm.shape
    got = jnp.concatenate([got_ref[:, 0, :], got_ref[:, 1, :]], axis=0)
    slot = got[:, rows : rows + 1] - 1.0
    lanes = iota((got.shape[0], column_count), 1).astype(F32)
    slots = (lanes == slot).astype(F32).astype(BF16)
    slots_ref[...] = slots
    placed_ref[...] = sum(dot_tn(term, slots) for term in thirds(got[:, 0:rows]))
    copies = [pltpu.make_async_copy(placed_ref, out_hbm.at[i], sems.at[i]) for i in range(count)]
    for copy in copies:
        copy.start()
    for copy in copies:
        copy.wait()


def maps_kernel(
    odd_ref, nb_hbm, slot_hbm, dyn_hbm, tend_hbm,
    self_ref, chip_ref, core_ref, send_ref, dyn_ref, tend_ref, slot_ref, nb_ref, sems,
):
    pairs = [(slot_hbm, slot_ref), (nb_hbm, nb_ref), (dyn_hbm, dyn_ref), (tend_hbm, tend_ref)]
    copies = [pltpu.make_async_copy(source, target, sems.at[i]) for i, (source, target) in enumerate(pairs)]
    for copy in copies:
        copy.start()
    copies[0].wait()
    copies[1].wait()
    maps(odd_ref, nb_ref, slot_ref, self_ref, chip_ref, core_ref, send_ref)
    for copy in copies[2:]:
        copy.wait()


def state_kernel(cells, whole_ref, crm_ref, left_hbm, right_hbm, left_ref, right_ref, sems):
    fields, size, _ = whole_ref.shape
    levels = left_ref.shape[2]
    for f in range(fields):
        for j in range(2):
            left_ref[j, f] = whole_ref[f, pl.ds(j, levels, stride=cells), :]
            right_ref[j, f] = whole_ref[f, pl.ds(cells - 2 + j, levels, stride=cells), :]
    copies = []
    for i, (near, far) in enumerate(((left_ref, left_hbm), (right_ref, right_hbm))):
        copies.append(pltpu.make_async_copy(near, far, sems.at[i]))
        copies[i].start()
    step = 64

    @pl.loop(0, size // step)
    def _(i):
        for f in range(fields):
            source = pl.ds(pl.multiple_of(i * step, 8), step)
            crm_ref[f, pl.ds(pl.multiple_of(PAD + i * step, 8), step), :] = whole_ref[f, source, :]

    for copy in copies:
        copy.wait()


def stack(ref, f, first, group, cells, levels):
    def level(k):
        return ref[f, pl.ds(pl.multiple_of(PAD + k * cells, 8), cells), :]

    below = jnp.where(first > 0, 1.0, 0.0) * level(jnp.maximum(first - 1, 0))
    above = jnp.where(first + group < levels, 1.0, 0.0) * level(jnp.minimum(first + group, levels - 1))
    west = [ref[f, pl.ds(PAD - 1 + (first + j) * cells, cells), :] for j in range(group)]
    east = [ref[f, pl.ds(PAD + 1 + (first + j) * cells, cells), :] for j in range(group)]
    return [below] + [level(first + j) for j in range(group)] + [above], west, east


def beside(west, east, west_end, east_end):
    cells = west.shape[0]
    cell = iota(west.shape, 0)
    return jnp.where(cell == 0, west_end, west), jnp.where(cell == cells - 1, east_end, east)


def shares(wind):
    speed = 0.5 * COURANT * jnp.tanh(wind)
    return DIFFUSE_X - speed, DIFFUSE_X + speed


def vertical(value):
    levels = value.shape[0]
    level = iota(value.shape, 0)
    up = jnp.where(level < levels - 1, pltpu.roll(value, levels - 1, 0), 0.0)
    down = jnp.where(level > 0, pltpu.roll(value, 1, 0), 0.0)
    return up + down


def folded(value):
    total = value[0:8]
    for i in range(8, value.shape[0], 8):
        total = total + value[i : i + 8]
    return total


def over_rows(ref, f, levels):
    total = ref[f, pl.ds(0, levels, stride=8), :]
    for i in range(1, 8):
        total = total + ref[f, pl.ds(i, levels, stride=8), :]
    return total


def first_kernel(cells, _, left_ref, right_ref, state_ref, end_ref, fold_ref, done_ref, old_ref):
    fields, levels, _ = end_ref.shape[1:]
    group = 4

    def column(cell):
        return [state_ref[f, pl.ds(PAD + cell, levels, stride=cells), :] for f in range(fields)]

    ends = [column(cell) for cell in (0, cells - 1)]
    for side in range(2):
        for f in range(fields):
            end_ref[side, f] = ends[side][f]

    def level_at(k, rows=cells):
        return pl.ds(pl.multiple_of(PAD + k * cells, 8), rows)

    old_ref[...] = jnp.zeros(old_ref.shape, F32)

    @pl.loop(0, levels // group)
    def _(step):
        first = step * group
        stacks = [stack(state_ref, f, first, group, cells, levels) for f in range(fields)]
        for j in range(group):
            k = first + j
            from_east, from_west = shares(stacks[0][0][j + 1])
            moved = []
            for f in range(fields):
                down, centre, up = stacks[f][0][j : j + 3]
                if j == 0:
                    down = old_ref[f]
                west, east = beside(
                    stacks[f][1][j], stacks[f][2][j], left_ref[1, f, pl.ds(k, 1), :], right_ref[0, f, pl.ds(k, 1), :]
                )
                fold_ref[f, pl.ds(pl.multiple_of(k * 8, 8), 8), :] = folded(centre)
                moved.append(CENTRE * centre + DIFFUSE_Z * (up + down) + from_east * east + from_west * west)
            for f, value in enumerate(physics(moved)):
                done_ref[f, j * cells : (j + 1) * cells] = value
        for f in range(fields):
            old_ref[f] = state_ref[f, level_at(first + group - 1), :]
            state_ref[f, level_at(first, group * cells), :] = done_ref[f]

    def halo(west, centre, east, side):
        from_east, from_west = shares(centre[0])
        moved = [
            CENTRE * centre[f] + DIFFUSE_Z * vertical(centre[f]) + from_east * east[f] + from_west * west[f]
            for f in range(fields)
        ]
        for f, value in enumerate(physics(moved)):
            end_ref[side, f] = value

    own = [[end_ref[side, f] for f in range(fields)] for side in range(2)]
    halo(left_ref[0], left_ref[1], own[0], 0)
    halo(own[1], right_ref[0], right_ref[1], 1)
    for f in range(fields):
        end_ref[2, f] = over_rows(fold_ref, f, levels)


def second_kernel(
    force_ref, pre_ref, end_ref, out_ref, part_ref, rest_ref, push_ref, shift_ref, next_ref, fold_ref, sems
):
    fields, levels, _ = end_ref.shape[1:]
    cells = out_ref.shape[1] // levels
    blocks = force_ref.shape[0]
    share = levels // blocks
    group = 4
    for f in range(fields):
        for b in range(blocks):
            push_ref[f, b * share : (b + 1) * share] = force_ref[b, f * share : (f + 1) * share]
    for f in range(fields):
        push = push_ref[f]
        shift_ref[f] = (1.0 - 2.0 * DIFFUSE_Z) * push + DIFFUSE_Z * vertical(push)
    copies = []
    for b in range(blocks):

        @pl.loop(0, share // group)
        def _(step):
            first = b * share + step * group
            stacks = [stack(pre_ref, f, first, group, cells, levels) for f in range(fields)]
            for j in range(group):
                k = first + j
                push = [push_ref[f, pl.ds(k, 1), :] for f in range(fields)]
                from_east, from_west = shares(stacks[0][0][j + 1] + push[0])
                moved = []
                for f in range(fields):
                    down, centre, up = stacks[f][0][j : j + 3]
                    west, east = beside(
                        stacks[f][1][j], stacks[f][2][j], end_ref[0, f, pl.ds(k, 1), :], end_ref[1, f, pl.ds(k, 1), :]
                    )
                    moved.append(
                        (CENTRE * centre + shift_ref[f, pl.ds(k, 1), :])
                        + DIFFUSE_Z * (up + down)
                        + from_east * east
                        + from_west * west
                    )
                for f, value in enumerate(physics(moved)):
                    value = value + push[f]
                    if b < blocks - 1:
                        next_ref[f, pl.ds(pl.multiple_of(k * cells, 8), cells), :] = value
                    else:
                        rest_ref[f, pl.ds(pl.multiple_of((k - b * share) * cells, 8), cells), :] = value
                    fold_ref[f, pl.ds(pl.multiple_of(k * 8, 8), 8), :] = folded(value)

        if b == blocks - 1:
            break
        here = pl.ds(b * share * cells, share * cells)
        copy = pltpu.make_async_copy(next_ref.at[:, here], out_ref.at[:, here], sems.at[b])
        copy.start()
        copies.append(copy)
    for f in range(fields):
        change = over_rows(fold_ref, f, levels) - end_ref[2, f]
        for b in range(blocks):
            part_ref[b, f * share : (f + 1) * share] = change[b * share : (b + 1) * share]
    for copy in copies:
        copy.wait()


def back_kernel(scale, part_ref, slots_ref, out_ref):
    blocks, rows, lanes = part_ref.shape
    total = part_ref[0]
    for b in range(1, blocks):
        total = total + part_ref[b]
    slots = slots_ref[...]
    message = 0.0
    for term in thirds(total * scale):
        message = message + dot_nt(slots, jnp.concatenate([term, term], axis=0))
    owners = message.shape[0] // 2
    first = iota((owners, 2 * rows), 1) < rows
    message = jnp.where(first, message[0:owners], message[owners:])
    turn = (FIRST - FIRST_BACK) % owners
    out_ref[turn:, 0, :] = message[0 : owners - turn]
    if turn > 0:
        out_ref[0:turn, 0, :] = message[owners - turn :]


def final_kernel(got_ref, send_ref, smooth_ref, rest_ref, _, dyn_hbm, crm_hbm, dyn_ref, sems):
    rows, columns = smooth_ref.shape
    size = rest_ref.shape[1]
    rest = pltpu.make_async_copy(rest_ref, crm_hbm.at[:, pl.ds(crm_hbm.shape[1] - size, size)], sems.at[0])
    rest.start()
    turn = (FIRST - FIRST_BACK) % got_ref.shape[0]
    got = got_ref[turn:, 0, :]
    if turn > 0:
        got = jnp.concatenate([got, got_ref[0:turn, 0, :]], axis=0)
    got = jnp.concatenate([got[:, 0:rows], got[:, rows:]], axis=0)
    dyn_ref[...] = smooth_ref[...] + sum(dot_tn(term, send_ref[...]) for term in thirds(got))
    copy = pltpu.make_async_copy(dyn_ref, dyn_hbm, sems.at[1])
    copy.start()
    rest.wait()
    copy.wait()


def call(kernel, outs, *args, scalars=(), far=(), scratch=(), same=None, cost=0, limit=4, name=None):
    vmem = pl.BlockSpec(memory_space=pltpu.VMEM)
    smem = pl.BlockSpec(memory_space=pltpu.SMEM)
    hbm = pl.BlockSpec(memory_space=pltpu.HBM)
    args = [pltpu.with_memory_space_constraint(a, pltpu.HBM) if i in far else a for i, a in enumerate(args)]
    return pl.pallas_call(
        kernel,
        out_shape=[s for s, _ in outs],
        in_specs=[smem if i in scalars else hbm if i in far else vmem for i in range(len(args))],
        out_specs=[hbm if distant else vmem for _, distant in outs],
        scratch_shapes=list(scratch),
        input_output_aliases=same or {},
        cost_estimate=pl.CostEstimate(flops=cost, bytes_accessed=0, transcendentals=0) if cost else None,
        compiler_params=pltpu.CompilerParams(vmem_limit_bytes=limit * 1024 * 1024),
        name=name,
    )(*args)


def near(*shape, dtype=F32):
    return (jax.ShapeDtypeStruct(shape, dtype), False)


def there(*shape, dtype=F32):
    return (pltpu.HBM(shape, dtype), True)


def per_device(crm_state, dyn_state, ls_tend, span_slot, neighbours):
    elem_count = lax.axis_size("elem")
    lev_count = lax.axis_size("lev")
    fields, share, columns = dyn_state.shape
    _, levels, cells, _ = crm_state.shape
    rows = fields * share
    dyn = dyn_state.reshape(rows, columns)
    tend = ls_tend.reshape(rows, columns)
    slot = span_slot.reshape(1, columns)
    crm_flat = crm_state.reshape(fields, levels * cells, columns)
    dma = pltpu.SemaphoreType.DMA

    core_pairs = [(i, i ^ 1) for i in range(elem_count)]
    chip_pairs = [(i, ((i ^ 1) + (2 if i & 1 else -2)) % elem_count) for i in range(elem_count)]
    from_chip = lax.ppermute(dyn, "elem", chip_pairs)

    odd = (lax.axis_index("elem") & 1).astype(jnp.int32).reshape(1, 1)
    square = near(columns, columns, dtype=BF16)
    padded = (fields, levels * cells + 2 * PAD, columns)
    edge = (2, fields, levels, columns)
    mself, mchip, mcore, send, dyn_near, tend_near, slot_near = call(
        maps_kernel,
        [
            square,
            square,
            square,
            near(2 * elem_count, columns, dtype=BF16),
            near(rows, columns),
            near(rows, columns),
            near(1, columns, dtype=jnp.int32),
        ],
        odd,
        neighbours.T,
        slot,
        dyn,
        tend,
        scalars=(0,),
        far=(1, 2, 3, 4),
        scratch=[pltpu.VMEM((4, columns // 4), jnp.int32), dma((4,))],
        cost=10**10,
        name="maps",
    )
    from_core = lax.ppermute(dyn_near, "elem", core_pairs)
    state, left, right = call(
        functools.partial(state_kernel, cells),
        [near(*padded), there(*edge), there(*edge)],
        crm_flat,
        scratch=[pltpu.VMEM(edge, F32), pltpu.VMEM(edge, F32), dma((2,))],
        name="state",
    )
    message, smoothed = call(
        forcing_kernel,
        [there(elem_count, 2, columns), near(rows, columns)],
        from_core,
        from_chip,
        dyn_near,
        tend_near,
        slot_near,
        mself,
        mchip,
        mcore,
        send,
        left,
        far=(9,),
        scratch=[pltpu.VMEM((elem_count, 2, columns), F32), dma((2,))],
        name="forcing",
    )
    order, order_back = [[[(first + i) % elem_count for i in range(elem_count)]] for first in (FIRST, FIRST_BACK)]
    got = lax.all_to_all(message, "elem", split_axis=0, concat_axis=0, axis_index_groups=order, tiled=True)

    ring = [(i, (i + 1) % lev_count) for i in range(lev_count)]
    from_left = lax.ppermute(right, "lev", ring)
    from_right = lax.ppermute(left, "lev", [(j, i) for i, j in ring])
    eighths = (fields, levels * 8, columns)
    pre, ends = call(
        functools.partial(first_kernel, cells),
        [near(*padded), near(3, fields, levels, columns)],
        state,
        from_left,
        from_right,
        scratch=[
            pltpu.VMEM(eighths, F32),
            pltpu.VMEM((fields, 4 * cells, columns), F32),
            pltpu.VMEM((fields, cells, columns), F32),
        ],
        same={0: 0},
        limit=8,
        name="first_substep",
    )

    placed, slots = call(
        place_kernel,
        [there(lev_count, rows, columns), near(2 * elem_count, columns, dtype=BF16)],
        got,
        scratch=[pltpu.VMEM((rows, columns), F32), dma((lev_count,))],
        name="place",
    )
    force = lax.all_to_all(placed, "lev", split_axis=0, concat_axis=0, tiled=True)
    size = levels // lev_count * cells
    crm_next, parts, rest = call(
        second_kernel,
        [there(fields, levels * cells, columns), near(lev_count, rows, columns), near(fields, size, columns)],
        force,
        pre,
        ends,
        scratch=[
            pltpu.VMEM((fields, levels, columns), F32),
            pltpu.VMEM((fields, levels, columns), F32),
            pltpu.VMEM((fields, levels * cells - size, columns), F32),
            pltpu.VMEM(eighths, F32),
            dma((lev_count - 1,)),
        ],
        limit=8,
        name="second_substep",
    )
    parts = lax.all_to_all(parts, "lev", split_axis=0, concat_axis=0, tiled=True)
    scale = 1.0 / (cells * lev_count * SUBSTEPS)
    (answer,) = call(
        functools.partial(back_kernel, scale),
        [near(elem_count, 1, 2 * rows)],
        parts,
        slots,
        name="back",
    )
    back = lax.all_to_all(answer, "elem", split_axis=0, concat_axis=0, axis_index_groups=order_back, tiled=True)
    dynamics, crm_next = call(
        final_kernel,
        [there(rows, columns), there(fields, levels * cells, columns)],
        back,
        send,
        smoothed,
        rest,
        crm_next,
        far=(4,),
        scratch=[pltpu.VMEM((rows, columns), F32), dma((2,))],
        same={4: 1},
        name="final",
    )
    return crm_next.reshape(crm_state.shape), dynamics.reshape(fields, share, columns)


def solution(mesh):
    return jax.shard_map(
        per_device,
        mesh=mesh,
        in_specs=(
            P(None, None, "lev", "elem"),
            P(None, "lev", "elem"),
            P(None, "lev", "elem"),
            P("elem"),
            P("elem", None),
        ),
        out_specs=(P(None, None, "lev", "elem"), P(None, "lev", "elem")),
        check_vma=False,
    )
```

```python
import functools

import jax
import jax.numpy as jnp
from jax import lax
from jax.experimental import pallas as pl
from jax.experimental.pallas import tpu as pltpu
from jax.sharding import PartitionSpec as P

SUBSTEPS = 2
SAT_ITERS = 3
DIFFUSE_X = 0.2
DIFFUSE_Z = 0.1
COURANT = 0.3
SAT_SLOPE = 0.3
LOG2_E = 1.4426950408889634
LATENT = 0.5
RELAX_RATE = 0.5
AUTOCONV = 0.2
BUOYANCY = 0.5
EDGE_WEIGHT = 0.25
CENTRE = 1.0 - 2.0 * DIFFUSE_X - 2.0 * DIFFUSE_Z

FIRST = 96
FIRST_BACK = 72
FIRST_LEV = 2

PAD = 8

F32 = jnp.float32
BF16 = jnp.bfloat16


def iota(shape, dim):
    return lax.broadcasted_iota(jnp.int32, shape, dim)


def thirds(x):
    high = x.astype(BF16)
    rest = x - high.astype(F32)
    middle = rest.astype(BF16)
    low = (rest - middle.astype(F32)).astype(BF16)
    return high, middle, low


def dot(a, b):
    return lax.dot_general(a, b, (((1,), (0,)), ((), ())), preferred_element_type=F32)


def dot_nt(a, b):
    return lax.dot_general(a, b, (((1,), (1,)), ((), ())), preferred_element_type=F32)


def dot_tn(a, b):
    return lax.dot_general(a, b, (((0,), (0,)), ((), ())), preferred_element_type=F32)


def physics(fields):
    wind_u, wind_w, temper, vapour, cloud_liq, cloud_ice, rain_water, snow_water = fields
    temper_start = temper
    for _ in range(SAT_ITERS):
        saturated = jnp.exp2(SAT_SLOPE * LOG2_E * temper)
        change = RELAX_RATE * (vapour - saturated) / (1.0 + LATENT * SAT_SLOPE * saturated)
        change = jnp.maximum(change, -cloud_liq)
        cloud_liq = cloud_liq + change
        vapour = vapour - change
        temper = temper + LATENT * change
    rainout = AUTOCONV * jnp.maximum(cloud_liq, 0.0)
    snowout = AUTOCONV * jnp.maximum(cloud_ice, 0.0)
    return [
        wind_u,
        wind_w + BUOYANCY * (temper - temper_start),
        temper,
        vapour,
        cloud_liq - rainout,
        cloud_ice - snowout,
        rain_water + rainout,
        snow_water + snowout,
    ]


def maps(odd_ref, nb_ref, slot_ref, self_ref, chip_ref, core_ref, send_ref):
    column_count = slot_ref.shape[1]
    elem_local = column_count // 4
    shape = (column_count, column_count)
    row, col = iota(shape, 0), iota(shape, 1)
    row_corner, col_corner = row & 3, col & 3
    spread = (iota((elem_local, column_count), 1) // 4 == iota((elem_local, column_count), 0)).astype(BF16)
    code = nb_ref[...]
    high = dot((code >> 7).astype(F32).astype(BF16), spread)
    low = dot((code & 127).astype(F32).astype(BF16), spread)
    code = (high * 128.0 + low).astype(jnp.int32)
    corner = iota((1, column_count), 1) & 3
    along_y = jnp.where(corner < 2, code[0:1], code[2:3])
    along_x = jnp.where((corner & 1) == 1, code[1:2], code[3:4])

    def partner(which):
        edge = which & 3
        place = (which >> 2) % elem_local
        touches = jnp.where(
            edge == 0,
            (row_corner < 2).astype(F32),
            jnp.where(
                edge == 1,
                (row_corner & 1).astype(F32),
                jnp.where(edge == 2, (row_corner >= 2).astype(F32), 1.0 - (row_corner & 1).astype(F32)),
            ),
        )
        return jnp.where((row >> 2) == place, touches, 0.0)

    weight = 0.5 * EDGE_WEIGHT
    own = ((row_corner >> 1) == (col_corner >> 1)).astype(F32) + ((row_corner & 1) == (col_corner & 1)).astype(F32)
    own = jnp.where((row >> 2) == (col >> 2), own, 0.0)
    self_ref[...] = (weight * (partner(along_y) - own)).astype(BF16)
    beside = weight * partner(along_x)
    from_core = (col_corner & 1) != odd_ref[0, 0]
    core_ref[...] = jnp.where(from_core, beside, 0.0).astype(BF16)
    chip_ref[...] = jnp.where(from_core, 0.0, beside).astype(BF16)

    spans = send_ref.shape[0] // 2
    goes = row == (slot_ref[...] // column_count + (spans - FIRST)) % spans
    onehot = goes.astype(F32).astype(BF16)
    rank = jnp.sum(jnp.where(row < col, dot_tn(onehot, onehot), 0.0), axis=0, keepdims=True)
    send_ref[0:column_count] = jnp.where(rank < 0.5, goes.astype(F32), 0.0).astype(BF16)
    send_ref[column_count:] = jnp.where(rank > 0.5, goes.astype(F32), 0.0).astype(BF16)


def forcing_kernel(
    core_ref, chip_ref, dyn_ref, ls_ref, slot_ref, mself, mchip, mcore, send_ref, _, out_hbm, smooth_ref, out_ref, sems
):
    rows, column_count = dyn_ref.shape
    dyn = dyn_ref[...]

    def through(value, matrix):
        return dot(jnp.concatenate(thirds(value), axis=0), matrix[...])

    change = through(dyn, mself) + through(core_ref[...], mcore) + through(chip_ref[...], mchip)
    change = change[0:rows] + change[rows : 2 * rows] + change[2 * rows :]
    smooth_ref[...] = dyn + change
    slot = ((slot_ref[...] % column_count) + 1).astype(F32)
    rest = column_count - rows
    extra = jnp.where(iota((rest, column_count), 0) == 0, slot, 0.0).astype(BF16)
    empty = jnp.zeros((rest, column_count), BF16)
    high, middle, low = thirds(ls_ref[...] + change)
    terms = [
        jnp.concatenate([high, extra], axis=0),
        jnp.concatenate([middle, empty], axis=0),
        jnp.concatenate([low, empty], axis=0),
    ]
    spans = send_ref.shape[0] // 2
    parts = sems.shape[0]
    size = spans // parts
    copies = []
    for part in range(parts):
        here = slice(part * size, (part + 1) * size)
        send = jnp.concatenate([send_ref[here], send_ref[spans + here.start : spans + here.stop]], axis=0)
        message = dot_nt(send, terms[0]) + dot_nt(send, terms[1]) + dot_nt(send, terms[2])
        out_ref[here, 0, :] = message[0:size]
        out_ref[here, 1, :] = message[size:]
        copies.append(pltpu.make_async_copy(out_ref.at[here], out_hbm.at[here], sems.at[part]))
        copies[part].start()
    for copy in copies:
        copy.wait()


def place_kernel(got_ref, out_hbm, slots_ref, placed_ref, sems):
    count, rows, column_count = out_hbm.shape
    got = jnp.concatenate([got_ref[:, 0, :], got_ref[:, 1, :]], axis=0)
    slot = got[:, rows : rows + 1] - 1.0
    lanes = iota((got.shape[0], column_count), 1).astype(F32)
    slots = (lanes == slot).astype(F32).astype(BF16)
    slots_ref[...] = slots
    placed_ref[...] = sum(dot_tn(term, slots) for term in thirds(got[:, 0:rows]))
    copies = [pltpu.make_async_copy(placed_ref, out_hbm.at[i], sems.at[i]) for i in range(count)]
    for copy in copies:
        copy.start()
    for copy in copies:
        copy.wait()


def maps_kernel(
    odd_ref, nb_hbm, slot_hbm, dyn_hbm, tend_hbm,
    self_ref, chip_ref, core_ref, send_ref, dyn_ref, tend_ref, slot_ref, nb_ref, sems,
):
    pairs = [(slot_hbm, slot_ref), (nb_hbm, nb_ref), (dyn_hbm, dyn_ref), (tend_hbm, tend_ref)]
    copies = [pltpu.make_async_copy(source, target, sems.at[i]) for i, (source, target) in enumerate(pairs)]
    for copy in copies:
        copy.start()
    copies[0].wait()
    copies[1].wait()
    maps(odd_ref, nb_ref, slot_ref, self_ref, chip_ref, core_ref, send_ref)
    for copy in copies[2:]:
        copy.wait()


def state_kernel(cells, whole_ref, crm_ref, left_hbm, right_hbm, left_ref, right_ref, sems):
    fields, size, _ = whole_ref.shape
    levels = left_ref.shape[2]
    for f in range(fields):
        for j in range(2):
            left_ref[j, f] = whole_ref[f, pl.ds(j, levels, stride=cells), :]
            right_ref[j, f] = whole_ref[f, pl.ds(cells - 2 + j, levels, stride=cells), :]
    copies = []
    for i, (near, far) in enumerate(((left_ref, left_hbm), (right_ref, right_hbm))):
        copies.append(pltpu.make_async_copy(near, far, sems.at[i]))
        copies[i].start()
    step = 64

    @pl.loop(0, size // step)
    def _(i):
        for f in range(fields):
            source = pl.ds(pl.multiple_of(i * step, 8), step)
            crm_ref[f, pl.ds(pl.multiple_of(PAD + i * step, 8), step), :] = whole_ref[f, source, :]

    for copy in copies:
        copy.wait()


def stack(ref, f, first, group, cells, levels):
    def level(k):
        return ref[f, pl.ds(pl.multiple_of(PAD + k * cells, 8), cells), :]

    below = jnp.where(first > 0, 1.0, 0.0) * level(jnp.maximum(first - 1, 0))
    above = jnp.where(first + group < levels, 1.0, 0.0) * level(jnp.minimum(first + group, levels - 1))
    west = [ref[f, pl.ds(PAD - 1 + (first + j) * cells, cells), :] for j in range(group)]
    east = [ref[f, pl.ds(PAD + 1 + (first + j) * cells, cells), :] for j in range(group)]
    return [below] + [level(first + j) for j in range(group)] + [above], west, east


def beside(west, east, west_end, east_end):
    cells = west.shape[0]
    cell = iota(west.shape, 0)
    return jnp.where(cell == 0, west_end, west), jnp.where(cell == cells - 1, east_end, east)


def shares(wind):
    speed = 0.5 * COURANT * jnp.tanh(wind)
    return DIFFUSE_X - speed, DIFFUSE_X + speed


def vertical(value):
    levels = value.shape[0]
    level = iota(value.shape, 0)
    up = jnp.where(level < levels - 1, pltpu.roll(value, levels - 1, 0), 0.0)
    down = jnp.where(level > 0, pltpu.roll(value, 1, 0), 0.0)
    return up + down


def folded(value):
    total = value[0:8]
    for i in range(8, value.shape[0], 8):
        total = total + value[i : i + 8]
    return total


def over_rows(ref, f, levels):
    total = ref[f, pl.ds(0, levels, stride=8), :]
    for i in range(1, 8):
        total = total + ref[f, pl.ds(i, levels, stride=8), :]
    return total


def first_kernel(cells, _, left_ref, right_ref, state_ref, end_ref, fold_ref, done_ref, old_ref):
    fields, levels, _ = end_ref.shape[1:]
    group = 4

    def column(cell):
        return [state_ref[f, pl.ds(PAD + cell, levels, stride=cells), :] for f in range(fields)]

    ends = [column(cell) for cell in (0, cells - 1)]
    for side in range(2):
        for f in range(fields):
            end_ref[side, f] = ends[side][f]

    def level_at(k, rows=cells):
        return pl.ds(pl.multiple_of(PAD + k * cells, 8), rows)

    old_ref[...] = jnp.zeros(old_ref.shape, F32)

    @pl.loop(0, levels // group)
    def _(step):
        first = step * group
        stacks = [stack(state_ref, f, first, group, cells, levels) for f in range(fields)]
        for j in range(group):
            k = first + j
            from_east, from_west = shares(stacks[0][0][j + 1])
            moved = []
            for f in range(fields):
                down, centre, up = stacks[f][0][j : j + 3]
                if j == 0:
                    down = old_ref[f]
                west, east = beside(
                    stacks[f][1][j], stacks[f][2][j], left_ref[1, f, pl.ds(k, 1), :], right_ref[0, f, pl.ds(k, 1), :]
                )
                fold_ref[f, pl.ds(pl.multiple_of(k * 8, 8), 8), :] = folded(centre)
                moved.append(CENTRE * centre + DIFFUSE_Z * (up + down) + from_east * east + from_west * west)
            for f, value in enumerate(physics(moved)):
                done_ref[f, j * cells : (j + 1) * cells] = value
        for f in range(fields):
            old_ref[f] = state_ref[f, level_at(first + group - 1), :]
            state_ref[f, level_at(first, group * cells), :] = done_ref[f]

    def halo(west, centre, east, side):
        from_east, from_west = shares(centre[0])
        moved = [
            CENTRE * centre[f] + DIFFUSE_Z * vertical(centre[f]) + from_east * east[f] + from_west * west[f]
            for f in range(fields)
        ]
        for f, value in enumerate(physics(moved)):
            end_ref[side, f] = value

    own = [[end_ref[side, f] for f in range(fields)] for side in range(2)]
    halo(left_ref[0], left_ref[1], own[0], 0)
    halo(own[1], right_ref[0], right_ref[1], 1)
    for f in range(fields):
        end_ref[2, f] = over_rows(fold_ref, f, levels)


def second_kernel(
    force_ref, pre_ref, end_ref, out_ref, part_ref, rest_ref, push_ref, shift_ref, next_ref, fold_ref, sems
):
    fields, levels, _ = end_ref.shape[1:]
    cells = out_ref.shape[1] // levels
    blocks = force_ref.shape[0]
    share = levels // blocks
    group = 4
    for f in range(fields):
        for b in range(blocks):
            push_ref[f, b * share : (b + 1) * share] = force_ref[(b - FIRST_LEV) % blocks, f * share : (f + 1) * share]
    for f in range(fields):
        push = push_ref[f]
        shift_ref[f] = (1.0 - 2.0 * DIFFUSE_Z) * push + DIFFUSE_Z * vertical(push)
    copies = []
    for b in range(blocks):

        @pl.loop(0, share // group)
        def _(step):
            first = b * share + step * group
            stacks = [stack(pre_ref, f, first, group, cells, levels) for f in range(fields)]
            for j in range(group):
                k = first + j
                push = [push_ref[f, pl.ds(k, 1), :] for f in range(fields)]
                from_east, from_west = shares(stacks[0][0][j + 1] + push[0])
                moved = []
                for f in range(fields):
                    down, centre, up = stacks[f][0][j : j + 3]
                    west, east = beside(
                        stacks[f][1][j], stacks[f][2][j], end_ref[0, f, pl.ds(k, 1), :], end_ref[1, f, pl.ds(k, 1), :]
                    )
                    moved.append(
                        (CENTRE * centre + shift_ref[f, pl.ds(k, 1), :])
                        + DIFFUSE_Z * (up + down)
                        + from_east * east
                        + from_west * west
                    )
                for f, value in enumerate(physics(moved)):
                    value = value + push[f]
                    if b < blocks - 1:
                        next_ref[f, pl.ds(pl.multiple_of(k * cells, 8), cells), :] = value
                    else:
                        rest_ref[f, pl.ds(pl.multiple_of((k - b * share) * cells, 8), cells), :] = value
                    fold_ref[f, pl.ds(pl.multiple_of(k * 8, 8), 8), :] = folded(value)

        if b == blocks - 1:
            break
        here = pl.ds(b * share * cells, share * cells)
        copy = pltpu.make_async_copy(next_ref.at[:, here], out_ref.at[:, here], sems.at[b])
        copy.start()
        copies.append(copy)
    for f in range(fields):
        change = over_rows(fold_ref, f, levels) - end_ref[2, f]
        for b in range(blocks):
            part_ref[(b - FIRST_LEV) % blocks, f * share : (f + 1) * share] = change[b * share : (b + 1) * share]
    for copy in copies:
        copy.wait()


def back_kernel(scale, part_ref, slots_ref, out_ref):
    blocks, rows, lanes = part_ref.shape
    total = part_ref[0]
    for b in range(1, blocks):
        total = total + part_ref[b]
    slots = slots_ref[...]
    message = 0.0
    for term in thirds(total * scale):
        message = message + dot_nt(slots, jnp.concatenate([term, term], axis=0))
    owners = message.shape[0] // 2
    first = iota((owners, 2 * rows), 1) < rows
    message = jnp.where(first, message[0:owners], message[owners:])
    turn = (FIRST - FIRST_BACK) % owners
    out_ref[turn:, 0, :] = message[0 : owners - turn]
    if turn > 0:
        out_ref[0:turn, 0, :] = message[owners - turn :]


def final_kernel(got_ref, send_ref, smooth_ref, rest_ref, _, dyn_hbm, crm_hbm, dyn_ref, sems):
    rows, columns = smooth_ref.shape
    size = rest_ref.shape[1]
    rest = pltpu.make_async_copy(rest_ref, crm_hbm.at[:, pl.ds(crm_hbm.shape[1] - size, size)], sems.at[0])
    rest.start()
    turn = (FIRST - FIRST_BACK) % got_ref.shape[0]
    got = got_ref[turn:, 0, :]
    if turn > 0:
        got = jnp.concatenate([got, got_ref[0:turn, 0, :]], axis=0)
    got = jnp.concatenate([got[:, 0:rows], got[:, rows:]], axis=0)
    dyn_ref[...] = smooth_ref[...] + sum(dot_tn(term, send_ref[...]) for term in thirds(got))
    copy = pltpu.make_async_copy(dyn_ref, dyn_hbm, sems.at[1])
    copy.start()
    rest.wait()
    copy.wait()


def call(kernel, outs, *args, scalars=(), far=(), scratch=(), same=None, cost=0, limit=4, name=None):
    vmem = pl.BlockSpec(memory_space=pltpu.VMEM)
    smem = pl.BlockSpec(memory_space=pltpu.SMEM)
    hbm = pl.BlockSpec(memory_space=pltpu.HBM)
    args = [pltpu.with_memory_space_constraint(a, pltpu.HBM) if i in far else a for i, a in enumerate(args)]
    return pl.pallas_call(
        kernel,
        out_shape=[s for s, _ in outs],
        in_specs=[smem if i in scalars else hbm if i in far else vmem for i in range(len(args))],
        out_specs=[hbm if distant else vmem for _, distant in outs],
        scratch_shapes=list(scratch),
        input_output_aliases=same or {},
        cost_estimate=pl.CostEstimate(flops=cost, bytes_accessed=0, transcendentals=0) if cost else None,
        compiler_params=pltpu.CompilerParams(vmem_limit_bytes=limit * 1024 * 1024),
        name=name,
    )(*args)


def near(*shape, dtype=F32):
    return (jax.ShapeDtypeStruct(shape, dtype), False)


def there(*shape, dtype=F32):
    return (pltpu.HBM(shape, dtype), True)


def per_device(crm_state, dyn_state, ls_tend, span_slot, neighbours):
    elem_count = lax.axis_size("elem")
    lev_count = lax.axis_size("lev")
    fields, share, columns = dyn_state.shape
    _, levels, cells, _ = crm_state.shape
    rows = fields * share
    dyn = dyn_state.reshape(rows, columns)
    tend = ls_tend.reshape(rows, columns)
    slot = span_slot.reshape(1, columns)
    crm_flat = crm_state.reshape(fields, levels * cells, columns)
    dma = pltpu.SemaphoreType.DMA

    core_pairs = [(i, i ^ 1) for i in range(elem_count)]
    chip_pairs = [(i, ((i ^ 1) + (2 if i & 1 else -2)) % elem_count) for i in range(elem_count)]
    from_chip = lax.ppermute(dyn, "elem", chip_pairs)

    odd = (lax.axis_index("elem") & 1).astype(jnp.int32).reshape(1, 1)
    square = near(columns, columns, dtype=BF16)
    padded = (fields, levels * cells + 2 * PAD, columns)
    edge = (2, fields, levels, columns)
    mself, mchip, mcore, send, dyn_near, tend_near, slot_near = call(
        maps_kernel,
        [
            square,
            square,
            square,
            near(2 * elem_count, columns, dtype=BF16),
            near(rows, columns),
            near(rows, columns),
            near(1, columns, dtype=jnp.int32),
        ],
        odd,
        neighbours.T,
        slot,
        dyn,
        tend,
        scalars=(0,),
        far=(1, 2, 3, 4),
        scratch=[pltpu.VMEM((4, columns // 4), jnp.int32), dma((4,))],
        cost=10**10,
        name="maps",
    )
    from_core = lax.ppermute(dyn_near, "elem", core_pairs)
    state, left, right = call(
        functools.partial(state_kernel, cells),
        [near(*padded), there(*edge), there(*edge)],
        crm_flat,
        scratch=[pltpu.VMEM(edge, F32), pltpu.VMEM(edge, F32), dma((2,))],
        name="state",
    )
    message, smoothed = call(
        forcing_kernel,
        [there(elem_count, 2, columns), near(rows, columns)],
        from_core,
        from_chip,
        dyn_near,
        tend_near,
        slot_near,
        mself,
        mchip,
        mcore,
        send,
        left,
        far=(9,),
        scratch=[pltpu.VMEM((elem_count, 2, columns), F32), dma((2,))],
        name="forcing",
    )
    order, order_back = [[[(first + i) % elem_count for i in range(elem_count)]] for first in (FIRST, FIRST_BACK)]
    got = lax.all_to_all(message, "elem", split_axis=0, concat_axis=0, axis_index_groups=order, tiled=True)

    ring = [(i, (i + 1) % lev_count) for i in range(lev_count)]
    from_left = lax.ppermute(right, "lev", ring)
    from_right = lax.ppermute(left, "lev", [(j, i) for i, j in ring])
    eighths = (fields, levels * 8, columns)
    pre, ends = call(
        functools.partial(first_kernel, cells),
        [near(*padded), near(3, fields, levels, columns)],
        state,
        from_left,
        from_right,
        scratch=[
            pltpu.VMEM(eighths, F32),
            pltpu.VMEM((fields, 4 * cells, columns), F32),
            pltpu.VMEM((fields, cells, columns), F32),
        ],
        same={0: 0},
        limit=8,
        name="first_substep",
    )

    placed, slots = call(
        place_kernel,
        [there(lev_count, rows, columns), near(2 * elem_count, columns, dtype=BF16)],
        got,
        scratch=[pltpu.VMEM((rows, columns), F32), dma((lev_count,))],
        name="place",
    )
    order_lev = [[(FIRST_LEV + i) % lev_count for i in range(lev_count)]]
    force = lax.all_to_all(placed, "lev", split_axis=0, concat_axis=0, axis_index_groups=order_lev, tiled=True)
    size = levels // lev_count * cells
    crm_next, parts, rest = call(
        second_kernel,
        [there(fields, levels * cells, columns), near(lev_count, rows, columns), near(fields, size, columns)],
        force,
        pre,
        ends,
        scratch=[
            pltpu.VMEM((fields, levels, columns), F32),
            pltpu.VMEM((fields, levels, columns), F32),
            pltpu.VMEM((fields, levels * cells - size, columns), F32),
            pltpu.VMEM(eighths, F32),
            dma((lev_count - 1,)),
        ],
        limit=8,
        name="second_substep",
    )
    parts = lax.all_to_all(parts, "lev", split_axis=0, concat_axis=0, axis_index_groups=order_lev, tiled=True)
    scale = 1.0 / (cells * lev_count * SUBSTEPS)
    (answer,) = call(
        functools.partial(back_kernel, scale),
        [near(elem_count, 1, 2 * rows)],
        parts,
        slots,
        name="back",
    )
    back = lax.all_to_all(answer, "elem", split_axis=0, concat_axis=0, axis_index_groups=order_back, tiled=True)
    dynamics, crm_next = call(
        final_kernel,
        [there(rows, columns), there(fields, levels * cells, columns)],
        back,
        send,
        smoothed,
        rest,
        crm_next,
        far=(4,),
        scratch=[pltpu.VMEM((rows, columns), F32), dma((2,))],
        same={4: 1},
        name="final",
    )
    return crm_next.reshape(crm_state.shape), dynamics.reshape(fields, share, columns)


def solution(mesh):
    return jax.shard_map(
        per_device,
        mesh=mesh,
        in_specs=(
            P(None, None, "lev", "elem"),
            P(None, "lev", "elem"),
            P(None, "lev", "elem"),
            P("elem"),
            P("elem", None),
        ),
        out_specs=(P(None, None, "lev", "elem"), P(None, "lev", "elem")),
        check_vma=False,
    )
```

```python
import functools

import jax
import jax.numpy as jnp
from jax import lax
from jax.experimental import pallas as pl
from jax.experimental.pallas import tpu as pltpu
from jax.sharding import PartitionSpec as P

SUBSTEPS = 2
SAT_ITERS = 3
DIFFUSE_X = 0.2
DIFFUSE_Z = 0.1
COURANT = 0.3
SAT_SLOPE = 0.3
LOG2_E = 1.4426950408889634
LATENT = 0.5
RELAX_RATE = 0.5
AUTOCONV = 0.2
BUOYANCY = 0.5
EDGE_WEIGHT = 0.25
CENTRE = 1.0 - 2.0 * DIFFUSE_X - 2.0 * DIFFUSE_Z

FIRST = 112
FIRST_BACK = 72
FIRST_LEV = 2

PAD = 8

F32 = jnp.float32
BF16 = jnp.bfloat16


def iota(shape, dim):
    return lax.broadcasted_iota(jnp.int32, shape, dim)


def thirds(x):
    high = x.astype(BF16)
    rest = x - high.astype(F32)
    middle = rest.astype(BF16)
    low = (rest - middle.astype(F32)).astype(BF16)
    return high, middle, low


def dot(a, b):
    return lax.dot_general(a, b, (((1,), (0,)), ((), ())), preferred_element_type=F32)


def dot_nt(a, b):
    return lax.dot_general(a, b, (((1,), (1,)), ((), ())), preferred_element_type=F32)


def dot_tn(a, b):
    return lax.dot_general(a, b, (((0,), (0,)), ((), ())), preferred_element_type=F32)


def physics(fields):
    wind_u, wind_w, temper, vapour, cloud_liq, cloud_ice, rain_water, snow_water = fields
    temper_start = temper
    for _ in range(SAT_ITERS):
        saturated = jnp.exp2(SAT_SLOPE * LOG2_E * temper)
        change = RELAX_RATE * (vapour - saturated) / (1.0 + LATENT * SAT_SLOPE * saturated)
        change = jnp.maximum(change, -cloud_liq)
        cloud_liq = cloud_liq + change
        vapour = vapour - change
        temper = temper + LATENT * change
    rainout = AUTOCONV * jnp.maximum(cloud_liq, 0.0)
    snowout = AUTOCONV * jnp.maximum(cloud_ice, 0.0)
    return [
        wind_u,
        wind_w + BUOYANCY * (temper - temper_start),
        temper,
        vapour,
        cloud_liq - rainout,
        cloud_ice - snowout,
        rain_water + rainout,
        snow_water + snowout,
    ]


def maps(odd_ref, nb_ref, slot_ref, self_ref, chip_ref, core_ref, send_ref):
    column_count = slot_ref.shape[1]
    elem_local = column_count // 4
    shape = (column_count, column_count)
    row, col = iota(shape, 0), iota(shape, 1)
    row_corner, col_corner = row & 3, col & 3
    spread = (iota((elem_local, column_count), 1) // 4 == iota((elem_local, column_count), 0)).astype(BF16)
    code = nb_ref[...]
    high = dot((code >> 7).astype(F32).astype(BF16), spread)
    low = dot((code & 127).astype(F32).astype(BF16), spread)
    code = (high * 128.0 + low).astype(jnp.int32)
    corner = iota((1, column_count), 1) & 3
    along_y = jnp.where(corner < 2, code[0:1], code[2:3])
    along_x = jnp.where((corner & 1) == 1, code[1:2], code[3:4])

    def partner(which):
        edge = which & 3
        place = (which >> 2) % elem_local
        touches = jnp.where(
            edge == 0,
            (row_corner < 2).astype(F32),
            jnp.where(
                edge == 1,
                (row_corner & 1).astype(F32),
                jnp.where(edge == 2, (row_corner >= 2).astype(F32), 1.0 - (row_corner & 1).astype(F32)),
            ),
        )
        return jnp.where((row >> 2) == place, touches, 0.0)

    weight = 0.5 * EDGE_WEIGHT
    own = ((row_corner >> 1) == (col_corner >> 1)).astype(F32) + ((row_corner & 1) == (col_corner & 1)).astype(F32)
    own = jnp.where((row >> 2) == (col >> 2), own, 0.0)
    self_ref[...] = (weight * (partner(along_y) - own)).astype(BF16)
    beside = weight * partner(along_x)
    from_core = (col_corner & 1) != odd_ref[0, 0]
    core_ref[...] = jnp.where(from_core, beside, 0.0).astype(BF16)
    chip_ref[...] = jnp.where(from_core, 0.0, beside).astype(BF16)

    spans = send_ref.shape[0] // 2
    goes = row == (slot_ref[...] // column_count + (spans - FIRST)) % spans
    onehot = goes.astype(F32).astype(BF16)
    rank = jnp.sum(jnp.where(row < col, dot_tn(onehot, onehot), 0.0), axis=0, keepdims=True)
    send_ref[0:column_count] = jnp.where(rank < 0.5, goes.astype(F32), 0.0).astype(BF16)
    send_ref[column_count:] = jnp.where(rank > 0.5, goes.astype(F32), 0.0).astype(BF16)


def forcing_kernel(
    core_ref, chip_ref, dyn_ref, ls_ref, slot_ref, mself, mchip, mcore, send_ref, _, out_hbm, smooth_ref, out_ref, sems
):
    rows, column_count = dyn_ref.shape
    dyn = dyn_ref[...]

    def through(value, matrix):
        return dot(jnp.concatenate(thirds(value), axis=0), matrix[...])

    change = through(dyn, mself) + through(core_ref[...], mcore) + through(chip_ref[...], mchip)
    change = change[0:rows] + change[rows : 2 * rows] + change[2 * rows :]
    smooth_ref[...] = dyn + change
    slot = ((slot_ref[...] % column_count) + 1).astype(F32)
    rest = column_count - rows
    extra = jnp.where(iota((rest, column_count), 0) == 0, slot, 0.0).astype(BF16)
    empty = jnp.zeros((rest, column_count), BF16)
    high, middle, low = thirds(ls_ref[...] + change)
    terms = [
        jnp.concatenate([high, extra], axis=0),
        jnp.concatenate([middle, empty], axis=0),
        jnp.concatenate([low, empty], axis=0),
    ]
    spans = send_ref.shape[0] // 2
    parts = sems.shape[0]
    size = spans // parts
    copies = []
    for part in range(parts):
        here = slice(part * size, (part + 1) * size)
        send = jnp.concatenate([send_ref[here], send_ref[spans + here.start : spans + here.stop]], axis=0)
        message = dot_nt(send, terms[0]) + dot_nt(send, terms[1]) + dot_nt(send, terms[2])
        out_ref[here, 0, :] = message[0:size]
        out_ref[here, 1, :] = message[size:]
        copies.append(pltpu.make_async_copy(out_ref.at[here], out_hbm.at[here], sems.at[part]))
        copies[part].start()
    for copy in copies:
        copy.wait()


def place_kernel(got_ref, out_hbm, slots_ref, placed_ref, sems):
    count, rows, column_count = out_hbm.shape
    got = jnp.concatenate([got_ref[:, 0, :], got_ref[:, 1, :]], axis=0)
    slot = got[:, rows : rows + 1] - 1.0
    lanes = iota((got.shape[0], column_count), 1).astype(F32)
    slots = (lanes == slot).astype(F32).astype(BF16)
    slots_ref[...] = slots
    placed_ref[...] = sum(dot_tn(term, slots) for term in thirds(got[:, 0:rows]))
    copies = [pltpu.make_async_copy(placed_ref, out_hbm.at[i], sems.at[i]) for i in range(count)]
    for copy in copies:
        copy.start()
    for copy in copies:
        copy.wait()


def maps_kernel(
    odd_ref, nb_hbm, slot_hbm, dyn_hbm, tend_hbm,
    self_ref, chip_ref, core_ref, send_ref, dyn_ref, tend_ref, slot_ref, nb_ref, sems,
):
    pairs = [(slot_hbm, slot_ref), (nb_hbm, nb_ref), (dyn_hbm, dyn_ref), (tend_hbm, tend_ref)]
    copies = [pltpu.make_async_copy(source, target, sems.at[i]) for i, (source, target) in enumerate(pairs)]
    for copy in copies:
        copy.start()
    copies[0].wait()
    copies[1].wait()
    maps(odd_ref, nb_ref, slot_ref, self_ref, chip_ref, core_ref, send_ref)
    for copy in copies[2:]:
        copy.wait()


def state_kernel(cells, whole_ref, crm_ref, left_hbm, right_hbm, left_ref, right_ref, sems):
    fields, size, _ = whole_ref.shape
    levels = left_ref.shape[2]
    for f in range(fields):
        for j in range(2):
            left_ref[j, f] = whole_ref[f, pl.ds(j, levels, stride=cells), :]
            right_ref[j, f] = whole_ref[f, pl.ds(cells - 2 + j, levels, stride=cells), :]
    copies = []
    for i, (near, far) in enumerate(((left_ref, left_hbm), (right_ref, right_hbm))):
        copies.append(pltpu.make_async_copy(near, far, sems.at[i]))
        copies[i].start()
    step = 64

    @pl.loop(0, size // step)
    def _(i):
        for f in range(fields):
            source = pl.ds(pl.multiple_of(i * step, 8), step)
            crm_ref[f, pl.ds(pl.multiple_of(PAD + i * step, 8), step), :] = whole_ref[f, source, :]

    for copy in copies:
        copy.wait()


def stack(ref, f, first, group, cells, levels):
    def level(k):
        return ref[f, pl.ds(pl.multiple_of(PAD + k * cells, 8), cells), :]

    below = jnp.where(first > 0, 1.0, 0.0) * level(jnp.maximum(first - 1, 0))
    above = jnp.where(first + group < levels, 1.0, 0.0) * level(jnp.minimum(first + group, levels - 1))
    west = [ref[f, pl.ds(PAD - 1 + (first + j) * cells, cells), :] for j in range(group)]
    east = [ref[f, pl.ds(PAD + 1 + (first + j) * cells, cells), :] for j in range(group)]
    return [below] + [level(first + j) for j in range(group)] + [above], west, east


def beside(west, east, west_end, east_end):
    cells = west.shape[0]
    cell = iota(west.shape, 0)
    return jnp.where(cell == 0, west_end, west), jnp.where(cell == cells - 1, east_end, east)


def shares(wind):
    speed = 0.5 * COURANT * jnp.tanh(wind)
    return DIFFUSE_X - speed, DIFFUSE_X + speed


def vertical(value):
    levels = value.shape[0]
    level = iota(value.shape, 0)
    up = jnp.where(level < levels - 1, pltpu.roll(value, levels - 1, 0), 0.0)
    down = jnp.where(level > 0, pltpu.roll(value, 1, 0), 0.0)
    return up + down


def folded(value):
    total = value[0:8]
    for i in range(8, value.shape[0], 8):
        total = total + value[i : i + 8]
    return total


def over_rows(ref, f, levels):
    total = ref[f, pl.ds(0, levels, stride=8), :]
    for i in range(1, 8):
        total = total + ref[f, pl.ds(i, levels, stride=8), :]
    return total


def first_kernel(cells, _, left_ref, right_ref, state_ref, end_ref, fold_ref, done_ref, old_ref):
    fields, levels, _ = end_ref.shape[1:]
    group = 4

    def column(cell):
        return [state_ref[f, pl.ds(PAD + cell, levels, stride=cells), :] for f in range(fields)]

    ends = [column(cell) for cell in (0, cells - 1)]
    for side in range(2):
        for f in range(fields):
            end_ref[side, f] = ends[side][f]

    def level_at(k, rows=cells):
        return pl.ds(pl.multiple_of(PAD + k * cells, 8), rows)

    old_ref[...] = jnp.zeros(old_ref.shape, F32)

    @pl.loop(0, levels // group)
    def _(step):
        first = step * group
        stacks = [stack(state_ref, f, first, group, cells, levels) for f in range(fields)]
        for j in range(group):
            k = first + j
            from_east, from_west = shares(stacks[0][0][j + 1])
            moved = []
            for f in range(fields):
                down, centre, up = stacks[f][0][j : j + 3]
                if j == 0:
                    down = old_ref[f]
                west, east = beside(
                    stacks[f][1][j], stacks[f][2][j], left_ref[1, f, pl.ds(k, 1), :], right_ref[0, f, pl.ds(k, 1), :]
                )
                fold_ref[f, pl.ds(pl.multiple_of(k * 8, 8), 8), :] = folded(centre)
                moved.append(CENTRE * centre + DIFFUSE_Z * (up + down) + from_east * east + from_west * west)
            for f, value in enumerate(physics(moved)):
                done_ref[f, j * cells : (j + 1) * cells] = value
        for f in range(fields):
            old_ref[f] = state_ref[f, level_at(first + group - 1), :]
            state_ref[f, level_at(first, group * cells), :] = done_ref[f]

    def halo(west, centre, east, side):
        from_east, from_west = shares(centre[0])
        moved = [
            CENTRE * centre[f] + DIFFUSE_Z * vertical(centre[f]) + from_east * east[f] + from_west * west[f]
            for f in range(fields)
        ]
        for f, value in enumerate(physics(moved)):
            end_ref[side, f] = value

    own = [[end_ref[side, f] for f in range(fields)] for side in range(2)]
    halo(left_ref[0], left_ref[1], own[0], 0)
    halo(own[1], right_ref[0], right_ref[1], 1)
    for f in range(fields):
        end_ref[2, f] = over_rows(fold_ref, f, levels)


def second_kernel(
    force_ref, pre_ref, end_ref, out_ref, part_ref, rest_ref, push_ref, shift_ref, next_ref, fold_ref, sems
):
    fields, levels, _ = end_ref.shape[1:]
    cells = out_ref.shape[1] // levels
    blocks = force_ref.shape[0]
    share = levels // blocks
    group = 4
    for f in range(fields):
        for b in range(blocks):
            push_ref[f, b * share : (b + 1) * share] = force_ref[(b - FIRST_LEV) % blocks, f * share : (f + 1) * share]
    for f in range(fields):
        push = push_ref[f]
        shift_ref[f] = (1.0 - 2.0 * DIFFUSE_Z) * push + DIFFUSE_Z * vertical(push)
    copies = []
    for b in range(blocks):

        @pl.loop(0, share // group)
        def _(step):
            first = b * share + step * group
            stacks = [stack(pre_ref, f, first, group, cells, levels) for f in range(fields)]
            for j in range(group):
                k = first + j
                push = [push_ref[f, pl.ds(k, 1), :] for f in range(fields)]
                from_east, from_west = shares(stacks[0][0][j + 1] + push[0])
                moved = []
                for f in range(fields):
                    down, centre, up = stacks[f][0][j : j + 3]
                    west, east = beside(
                        stacks[f][1][j], stacks[f][2][j], end_ref[0, f, pl.ds(k, 1), :], end_ref[1, f, pl.ds(k, 1), :]
                    )
                    moved.append(
                        (CENTRE * centre + shift_ref[f, pl.ds(k, 1), :])
                        + DIFFUSE_Z * (up + down)
                        + from_east * east
                        + from_west * west
                    )
                for f, value in enumerate(physics(moved)):
                    value = value + push[f]
                    if b < blocks - 1:
                        next_ref[f, pl.ds(pl.multiple_of(k * cells, 8), cells), :] = value
                    else:
                        rest_ref[f, pl.ds(pl.multiple_of((k - b * share) * cells, 8), cells), :] = value
                    fold_ref[f, pl.ds(pl.multiple_of(k * 8, 8), 8), :] = folded(value)

        if b == blocks - 1:
            break
        here = pl.ds(b * share * cells, share * cells)
        copy = pltpu.make_async_copy(next_ref.at[:, here], out_ref.at[:, here], sems.at[b])
        copy.start()
        copies.append(copy)
    for f in range(fields):
        change = over_rows(fold_ref, f, levels) - end_ref[2, f]
        for b in range(blocks):
            part_ref[(b - FIRST_LEV) % blocks, f * share : (f + 1) * share] = change[b * share : (b + 1) * share]
    for copy in copies:
        copy.wait()


def back_kernel(scale, part_ref, slots_ref, out_ref):
    blocks, rows, lanes = part_ref.shape
    total = part_ref[0]
    for b in range(1, blocks):
        total = total + part_ref[b]
    slots = slots_ref[...]
    message = 0.0
    for term in thirds(total * scale):
        message = message + dot_nt(slots, jnp.concatenate([term, term], axis=0))
    owners = message.shape[0] // 2
    first = iota((owners, 2 * rows), 1) < rows
    message = jnp.where(first, message[0:owners], message[owners:])
    turn = (FIRST - FIRST_BACK) % owners
    out_ref[turn:, 0, :] = message[0 : owners - turn]
    if turn > 0:
        out_ref[0:turn, 0, :] = message[owners - turn :]


def final_kernel(got_ref, send_ref, smooth_ref, rest_ref, _, dyn_hbm, crm_hbm, dyn_ref, sems):
    rows, columns = smooth_ref.shape
    size = rest_ref.shape[1]
    rest = pltpu.make_async_copy(rest_ref, crm_hbm.at[:, pl.ds(crm_hbm.shape[1] - size, size)], sems.at[0])
    rest.start()
    turn = (FIRST - FIRST_BACK) % got_ref.shape[0]
    got = got_ref[turn:, 0, :]
    if turn > 0:
        got = jnp.concatenate([got, got_ref[0:turn, 0, :]], axis=0)
    got = jnp.concatenate([got[:, 0:rows], got[:, rows:]], axis=0)
    dyn_ref[...] = smooth_ref[...] + sum(dot_tn(term, send_ref[...]) for term in thirds(got))
    copy = pltpu.make_async_copy(dyn_ref, dyn_hbm, sems.at[1])
    copy.start()
    rest.wait()
    copy.wait()


def call(kernel, outs, *args, scalars=(), far=(), scratch=(), same=None, cost=0, limit=4, name=None):
    vmem = pl.BlockSpec(memory_space=pltpu.VMEM)
    smem = pl.BlockSpec(memory_space=pltpu.SMEM)
    hbm = pl.BlockSpec(memory_space=pltpu.HBM)
    args = [pltpu.with_memory_space_constraint(a, pltpu.HBM) if i in far else a for i, a in enumerate(args)]
    return pl.pallas_call(
        kernel,
        out_shape=[s for s, _ in outs],
        in_specs=[smem if i in scalars else hbm if i in far else vmem for i in range(len(args))],
        out_specs=[hbm if distant else vmem for _, distant in outs],
        scratch_shapes=list(scratch),
        input_output_aliases=same or {},
        cost_estimate=pl.CostEstimate(flops=cost, bytes_accessed=0, transcendentals=0) if cost else None,
        compiler_params=pltpu.CompilerParams(vmem_limit_bytes=limit * 1024 * 1024),
        name=name,
    )(*args)


def near(*shape, dtype=F32):
    return (jax.ShapeDtypeStruct(shape, dtype), False)


def there(*shape, dtype=F32):
    return (pltpu.HBM(shape, dtype), True)


def per_device(crm_state, dyn_state, ls_tend, span_slot, neighbours):
    elem_count = lax.axis_size("elem")
    lev_count = lax.axis_size("lev")
    fields, share, columns = dyn_state.shape
    _, levels, cells, _ = crm_state.shape
    rows = fields * share
    dyn = dyn_state.reshape(rows, columns)
    tend = ls_tend.reshape(rows, columns)
    slot = span_slot.reshape(1, columns)
    crm_flat = crm_state.reshape(fields, levels * cells, columns)
    dma = pltpu.SemaphoreType.DMA

    core_pairs = [(i, i ^ 1) for i in range(elem_count)]
    chip_pairs = [(i, ((i ^ 1) + (2 if i & 1 else -2)) % elem_count) for i in range(elem_count)]
    from_chip = lax.ppermute(dyn, "elem", chip_pairs)

    odd = (lax.axis_index("elem") & 1).astype(jnp.int32).reshape(1, 1)
    square = near(columns, columns, dtype=BF16)
    padded = (fields, levels * cells + 2 * PAD, columns)
    edge = (2, fields, levels, columns)
    mself, mchip, mcore, send, dyn_near, tend_near, slot_near = call(
        maps_kernel,
        [
            square,
            square,
            square,
            near(2 * elem_count, columns, dtype=BF16),
            near(rows, columns),
            near(rows, columns),
            near(1, columns, dtype=jnp.int32),
        ],
        odd,
        neighbours.T,
        slot,
        dyn,
        tend,
        scalars=(0,),
        far=(1, 2, 3, 4),
        scratch=[pltpu.VMEM((4, columns // 4), jnp.int32), dma((4,))],
        cost=10**10,
        name="maps",
    )
    from_core = lax.ppermute(dyn_near, "elem", core_pairs)
    state, left, right = call(
        functools.partial(state_kernel, cells),
        [near(*padded), there(*edge), there(*edge)],
        crm_flat,
        scratch=[pltpu.VMEM(edge, F32), pltpu.VMEM(edge, F32), dma((2,))],
        name="state",
    )
    message, smoothed = call(
        forcing_kernel,
        [there(elem_count, 2, columns), near(rows, columns)],
        from_core,
        from_chip,
        dyn_near,
        tend_near,
        slot_near,
        mself,
        mchip,
        mcore,
        send,
        left,
        far=(9,),
        scratch=[pltpu.VMEM((elem_count, 2, columns), F32), dma((2,))],
        name="forcing",
    )
    order, order_back = [[[(first + i) % elem_count for i in range(elem_count)]] for first in (FIRST, FIRST_BACK)]
    got = lax.all_to_all(message, "elem", split_axis=0, concat_axis=0, axis_index_groups=order, tiled=True)

    ring = [(i, (i + 1) % lev_count) for i in range(lev_count)]
    from_left = lax.ppermute(right, "lev", ring)
    from_right = lax.ppermute(left, "lev", [(j, i) for i, j in ring])
    eighths = (fields, levels * 8, columns)
    pre, ends = call(
        functools.partial(first_kernel, cells),
        [near(*padded), near(3, fields, levels, columns)],
        state,
        from_left,
        from_right,
        scratch=[
            pltpu.VMEM(eighths, F32),
            pltpu.VMEM((fields, 4 * cells, columns), F32),
            pltpu.VMEM((fields, cells, columns), F32),
        ],
        same={0: 0},
        limit=8,
        name="first_substep",
    )

    placed, slots = call(
        place_kernel,
        [there(lev_count, rows, columns), near(2 * elem_count, columns, dtype=BF16)],
        got,
        scratch=[pltpu.VMEM((rows, columns), F32), dma((lev_count,))],
        name="place",
    )
    order_lev = [[(FIRST_LEV + i) % lev_count for i in range(lev_count)]]
    force = lax.all_to_all(placed, "lev", split_axis=0, concat_axis=0, axis_index_groups=order_lev, tiled=True)
    size = levels // lev_count * cells
    crm_next, parts, rest = call(
        second_kernel,
        [there(fields, levels * cells, columns), near(lev_count, rows, columns), near(fields, size, columns)],
        force,
        pre,
        ends,
        scratch=[
            pltpu.VMEM((fields, levels, columns), F32),
            pltpu.VMEM((fields, levels, columns), F32),
            pltpu.VMEM((fields, levels * cells - size, columns), F32),
            pltpu.VMEM(eighths, F32),
            dma((lev_count - 1,)),
        ],
        limit=8,
        name="second_substep",
    )
    parts = lax.all_to_all(parts, "lev", split_axis=0, concat_axis=0, axis_index_groups=order_lev, tiled=True)
    scale = 1.0 / (cells * lev_count * SUBSTEPS)
    (answer,) = call(
        functools.partial(back_kernel, scale),
        [near(elem_count, 1, 2 * rows)],
        parts,
        slots,
        name="back",
    )
    back = lax.all_to_all(answer, "elem", split_axis=0, concat_axis=0, axis_index_groups=order_back, tiled=True)
    dynamics, crm_next = call(
        final_kernel,
        [there(rows, columns), there(fields, levels * cells, columns)],
        back,
        send,
        smoothed,
        rest,
        crm_next,
        far=(4,),
        scratch=[pltpu.VMEM((rows, columns), F32), dma((2,))],
        same={4: 1},
        name="final",
    )
    return crm_next.reshape(crm_state.shape), dynamics.reshape(fields, share, columns)


def solution(mesh):
    return jax.shard_map(
        per_device,
        mesh=mesh,
        in_specs=(
            P(None, None, "lev", "elem"),
            P(None, "lev", "elem"),
            P(None, "lev", "elem"),
            P("elem"),
            P("elem", None),
        ),
        out_specs=(P(None, None, "lev", "elem"), P(None, "lev", "elem")),
        check_vma=False,
    )
```
